512 devices in a mesh: img: 16 (over z), unit: 32 (over y, x, core).
Axes of the slice: x: 4, y: 4, z: 16, core: 2. Of those that a mesh axis runs over, the one named last changes fastest.
Arguments:
- tokens: bfloat16 [16, 768, 16, 288], P('img', 'unit'), may hold values from -6 to 6
- live: int32 [16, 32], P('img', 'unit'), may hold values from 0 to 24, as said below
- cotangent: bfloat16 [16, 384, 4, 576], P('img', 'unit'), may hold values from -6 to 6
- w_qkv: bfloat16 [288, 864], replicated, may hold values from -0.375 to 0.375
- w_out: bfloat16 [288, 288], replicated, may hold values from -0.375 to 0.375
- w_pool: bfloat16 [288, 576], replicated, may hold values from -0.375 to 0.375
- gain_one: float32 [288], replicated, may hold values from 0.1 to 1.9
- gain_two: float32 [288], replicated, may hold values from 0.1 to 1.9
Outputs:
- pooled: bfloat16 [16, 384, 4, 576], P('img', 'unit')
- grad_tokens: bfloat16 [16, 768, 16, 288], P('img', 'unit')
- grad_qkv: float32 [288, 864], replicated
- grad_out: float32 [288, 288], replicated
- grad_pool: float32 [288, 576], replicated
- grad_gain_one: float32 [288], replicated
- grad_gain_two: float32 [288], replicated
The draws below stay inside these ranges and needn't reach their ends.
Inputs may be any that keep to these rules, and one draw needn't show every extreme that they name: The counts of an image sum to 384; for every unit shard j, the kept units before it, start = live[i, 0] + ... + live[i, j-1], number between j * 12 and (j + 1) * 12.
All inputs are finite; a program needn't handle non-finite values.
Results may differ from the reference program's by a relative error of at most 0.009.
Values may be sent and summed in bfloat16 or wider, within the bound.
A program may use at most 64 MiB of HBM per device.

```python
import math
import jax
import jax.numpy as jnp
from jax import lax

C2 = 288
C3 = 576
HEADS = 4
HEAD_DIM = 72
UNIT_TOKENS = 16
OUT = 12
SLOTS = 24
KEPT = 384
IMAGES = 16
N_UNIT = 32


def draw_live(key, part):
    key = jax.random.fold_in(key, 11)
    first_key, second_key = jax.random.split(key)
    excess = jax.random.randint(first_key, (IMAGES, N_UNIT), 0, OUT + 1)
    chosen = jax.random.randint(second_key, (IMAGES, 1), 1, N_UNIT - 1)
    column = jnp.arange(N_UNIT)[None, :]
    excess = jnp.where(column == chosen, OUT, excess)
    excess = jnp.where((column == chosen - 1) | (column == chosen + 1) | (column == N_UNIT - 1), 0, excess)
    before = jnp.concatenate([jnp.zeros((IMAGES, 1), excess.dtype), excess[:, :-1]], axis=1)
    return (OUT + excess - before).astype(jnp.int32)


def shard_levels(stream_key, dims, shards, smallest, largest):
    loudness = 1.0
    for position, parts in shards:
        heights = jax.random.uniform(jax.random.fold_in(jax.random.fold_in(stream_key, 6), position), (parts,), jnp.float32, smallest / len(shards), largest / len(shards))
        loudness = loudness * jnp.repeat(jnp.exp(heights), dims[position] // parts).reshape((-1,) + (1,) * (len(dims) - 1 - position))
    return loudness


def gaussian(own_key, shape, spread, reach, shards=(), kind=jnp.bfloat16):
    factor_of = shard_levels(own_key, shape, shards, -0.22, 0.18) if shards else 1.0
    drawn = jax.random.normal(own_key, shape, jnp.float32) * spread * factor_of
    return jnp.minimum(jnp.maximum(drawn, -reach), reach).astype(kind)


def setup_inputs(seed: int = 0) -> dict:
    keys = jax.random.split(jax.random.key(seed), 9)
    tokens = gaussian(keys[0], (IMAGES, N_UNIT * SLOTS, UNIT_TOKENS, C2), 1.0, 6.0, ((0, 16), (1, 32)))
    live = draw_live(jax.random.fold_in(keys[8], 71), 0)
    cotangent = gaussian(keys[2], (IMAGES, KEPT, UNIT_TOKENS // 4, C3), 1.0, 6.0, ((0, 16), (1, 32)))
    w_qkv = gaussian(keys[3], (C2, 3 * C2), C2 ** -0.5, 0.375)
    w_out = gaussian(keys[4], (C2, C2), C2 ** -0.5, 0.375)
    w_pool = gaussian(keys[5], (C2, C3), C2 ** -0.5, 0.375)
    gain_one = jnp.clip(1.0 + 0.18 * jax.random.normal(keys[6], (C2,), jnp.float32), 0.1, 1.9)
    gain_two = jnp.clip(1.0 + 0.18 * jax.random.normal(keys[7], (C2,), jnp.float32), 0.1, 1.9)
    return {"tokens": tokens, "live": live, "cotangent": cotangent, "w_qkv": w_qkv, "w_out": w_out, "w_pool": w_pool, "gain_one": gain_one, "gain_two": gain_two}


EPSILON = 1e-06

def normalize(values):
    average = lax.optimization_barrier(jnp.mean(values, axis=-1, keepdims=True))
    centred = values - average
    inv_scale = lax.rsqrt(lax.optimization_barrier(jnp.mean(centred * centred, axis=-1, keepdims=True)) + EPSILON)
    return (centred * inv_scale, inv_scale)

def norm_back(grad_norm, normed_v, inv_scale):
    first = lax.optimization_barrier(jnp.mean(grad_norm, axis=-1, keepdims=True))
    second = lax.optimization_barrier(jnp.mean(grad_norm * normed_v, axis=-1, keepdims=True))
    return inv_scale * (grad_norm - first - normed_v * second)

def pool_grid(values):
    unit_count, width = (values.shape[0], values.shape[-1])
    return lax.optimization_barrier(jnp.mean(values.reshape(unit_count, 2, 2, 2, 2, width), axis=(2, 4))).reshape(unit_count, 4, width)

def spread_grid(values):
    unit_count, width = (values.shape[0], values.shape[-1])
    grid = jnp.broadcast_to(values.reshape(unit_count, 2, 1, 2, 1, width), (unit_count, 2, 2, 2, 2, width))
    return grid.reshape(unit_count, 16, width) * 0.25

def mult(form, left, right):
    return jnp.einsum(form, left.astype(jnp.float32), right.astype(jnp.float32))

def forward(unit_rows, w_qkv, w_out, w_pool, gain_one, gain_two):
    unit_count, token_count, width = unit_rows.shape
    tokens_f = unit_rows.astype(jnp.float32)
    norm_one, scale_one = normalize(tokens_f)
    normed = (norm_one * gain_one).astype(jnp.bfloat16)
    proj_qkv = jnp.dot(normed.reshape(-1, width), w_qkv, preferred_element_type=jnp.float32).astype(jnp.bfloat16)
    proj_qkv = proj_qkv.reshape(unit_count, token_count, 3, HEADS, HEAD_DIM)
    query_part, key_part, value_part = (proj_qkv[:, :, 0], proj_qkv[:, :, 1], proj_qkv[:, :, 2])
    factor = HEAD_DIM ** (-0.5)
    scores = mult('uthd,ushd->uhts', query_part, key_part) * factor
    attend = jax.nn.softmax(scores, axis=-1)
    attend_b = attend.astype(jnp.bfloat16)
    mixed_heads = mult('uhts,ushd->uthd', attend_b, value_part).astype(jnp.bfloat16).reshape(unit_count, token_count, width)
    residual = tokens_f + jnp.dot(mixed_heads.reshape(-1, width), w_out, preferred_element_type=jnp.float32).reshape(unit_count, token_count, width)
    norm_two, scale_two = normalize(residual)
    grouped = pool_grid(norm_two * gain_two).astype(jnp.bfloat16)
    pooled = jnp.dot(grouped.reshape(-1, width), w_pool, preferred_element_type=jnp.float32).astype(jnp.bfloat16)
    pooled = pooled.reshape(unit_count, 4, w_pool.shape[1])
    saved = (norm_one, scale_one, normed, query_part, key_part, value_part, attend, attend_b, mixed_heads, norm_two, scale_two, grouped)
    return (pooled, saved)

def backward(saved, cotangent, w_qkv, w_out, w_pool, gain_one, gain_two):
    norm_one, scale_one, normed, query_part, key_part, value_part, attend, attend_b, mixed_heads, norm_two, scale_two, grouped = saved
    unit_count, token_count, width = norm_one.shape
    out_width = w_pool.shape[1]
    factor = HEAD_DIM ** (-0.5)
    cot_rows = cotangent.reshape(-1, out_width)
    grad_pool = jnp.dot(grouped.reshape(-1, width).T, cot_rows, preferred_element_type=jnp.float32)
    grad_grouped = jnp.dot(cot_rows, w_pool.T, preferred_element_type=jnp.float32).reshape(unit_count, 4, width)
    grad_scaled = spread_grid(grad_grouped)
    grad_gain_two = lax.optimization_barrier(jnp.sum(grad_scaled * norm_two, axis=(0, 1)))
    grad_resid = norm_back(grad_scaled * gain_two, norm_two, scale_two)
    resid_b = grad_resid.astype(jnp.bfloat16).reshape(-1, width)
    grad_out = jnp.dot(mixed_heads.reshape(-1, width).T, resid_b, preferred_element_type=jnp.float32)
    grad_mixed = jnp.dot(resid_b, w_out.T, preferred_element_type=jnp.float32).astype(jnp.bfloat16)
    grad_mixed = grad_mixed.reshape(unit_count, token_count, HEADS, HEAD_DIM)
    grad_attend = mult('uthd,ushd->uhts', grad_mixed, value_part)
    grad_value = mult('uhts,uthd->ushd', attend_b, grad_mixed).astype(jnp.bfloat16)
    grad_scores = (attend * (grad_attend - lax.optimization_barrier(jnp.sum(grad_attend * attend, axis=-1, keepdims=True))) * factor).astype(jnp.bfloat16)
    grad_query = mult('uhts,ushd->uthd', grad_scores, key_part).astype(jnp.bfloat16)
    grad_key = mult('uhts,uthd->ushd', grad_scores, query_part).astype(jnp.bfloat16)
    grad_proj = jnp.stack([grad_query, grad_key, grad_value], axis=2).reshape(-1, 3 * width)
    grad_qkv = jnp.dot(normed.reshape(-1, width).T, grad_proj, preferred_element_type=jnp.float32)
    grad_normed = jnp.dot(grad_proj, w_qkv.T, preferred_element_type=jnp.float32).reshape(unit_count, token_count, width)
    grad_gain_one = lax.optimization_barrier(jnp.sum(grad_normed * norm_one, axis=(0, 1)))
    grad_input = norm_back(grad_normed * gain_one, norm_one, scale_one)
    grad_tokens = (grad_resid + grad_input).astype(jnp.bfloat16)
    return (grad_tokens, (grad_qkv, grad_out, grad_pool, grad_gain_one, grad_gain_two))

def reference(tokens, live, cotangent, w_qkv, w_out, w_pool, gain_one, gain_two):

    def one_image(inputs):
        tokens_img, live_img, cot_img = inputs
        offsets = jnp.cumsum(live_img, dtype=jnp.int32) - live_img
        rank_ids = jnp.arange(KEPT, dtype=jnp.int32)
        owner_dev = lax.optimization_barrier(jnp.sum((offsets[None, 1:] <= rank_ids[:, None]).astype(jnp.int32), axis=1, dtype=jnp.int32))
        slot_ids = (owner_dev * SLOTS + rank_ids - jnp.take(offsets, owner_dev)).astype(jnp.int32)
        unit_rows = jnp.take(tokens_img, slot_ids, axis=0)
        pooled, saved = forward(unit_rows, w_qkv, w_out, w_pool, gain_one, gain_two)
        grad_units, grads = backward(saved, cot_img, w_qkv, w_out, w_pool, gain_one, gain_two)
        grad_slots = jnp.zeros(tokens_img.shape, jnp.bfloat16).at[slot_ids].set(grad_units)
        return (pooled, grad_slots, grads)
    pooled, grad_tokens, grads = lax.map(one_image, (tokens, live, cotangent))
    factor = 1.0 / math.sqrt(IMAGES * KEPT)
    totals = [lax.optimization_barrier(jnp.sum(item, axis=0)) * factor for item in grads]
    return (pooled, grad_tokens, totals[0], totals[1], totals[2], totals[3], totals[4])
```

```python
import functools
import math

import jax
import jax.numpy as jnp
from jax import lax
from jax.experimental import pallas as pl
from jax.experimental.pallas import tpu as pltpu
from jax.sharding import PartitionSpec as P

HEADS = 4
HEAD_DIM = 72
EPSILON = 1e-06
BF = jnp.bfloat16
F32 = jnp.float32
MESH = pl.DeviceIdType.MESH
TOK = 16
BLK = 128
LANES = 128
HALF = 2048
VMEM_LIMIT = 50 * 1024 * 1024


def nn(a, b):
    return lax.dot_general(a, b, (((1,), (0,)), ((), ())), preferred_element_type=F32)


def nt(a, b):
    return lax.dot_general(a, b, (((1,), (1,)), ((), ())), preferred_element_type=F32)


def tn(a, b):
    return lax.dot_general(a, b, (((0,), (0,)), ((), ())), preferred_element_type=F32)


def normalize(values):
    centred = values - jnp.mean(values, axis=-1, keepdims=True)
    inv_scale = lax.rsqrt(jnp.mean(centred * centred, axis=-1, keepdims=True) + EPSILON)
    return centred * inv_scale, inv_scale


def norm_back(grad_norm, normed_v, inv_scale):
    first = jnp.mean(grad_norm, axis=-1, keepdims=True)
    second = jnp.mean(grad_norm * normed_v, axis=-1, keepdims=True)
    return inv_scale * (grad_norm - first - normed_v * second)


def selection(shape, token_dim, shift, live):
    token = lax.broadcasted_iota(jnp.int32, shape, token_dim)
    row = lax.broadcasted_iota(jnp.int32, shape, 1 - token_dim)
    slot = token >> 4
    group = ((token >> 3) & 1) * 2 + ((token >> 1) & 1)
    hit = (row == (shift + slot) * 4 + group) & (slot < live)
    return jnp.where(hit, 0.25, 0.0).astype(BF)


def head_rows(block):
    lane = lax.broadcasted_iota(jnp.int32, (1, block.shape[1]), 1)
    parts = []
    for head in range(HEADS):
        mine = (lane >= head * HEAD_DIM) & (lane < (head + 1) * HEAD_DIM)
        parts.append(block * jnp.where(mine, 1.0, 0.0).astype(BF))
    return jnp.concatenate(parts, axis=0)


def heads_to_lanes(rows):
    return jnp.concatenate([rows[h * BLK : (h + 1) * BLK] for h in range(HEADS)], axis=1)


def gain_rows(total):
    row = lax.broadcasted_iota(jnp.int32, (32, LANES), 0)
    last = jnp.concatenate([total[:, 256:], jnp.zeros((1, 96), F32)], axis=1)
    out = jnp.where(row == 0, total[:, :128], 0.0)
    out = jnp.where(row == 1, total[:, 128:256], out)
    return jnp.where(row == 2, last, out).astype(BF)


def compute_kernel(
    live_ref, counts_ref, tokens_ref, cot_ref, next_ref, w_qkv_ref, w_out_ref, w_pool_ref, gain_one_ref, gain_two_ref,
    grad_tokens_ref, pooled_ref, g_ref, n_one_ref, n_two_ref, gr_ref, qkv_ref, mixed_ref, gqkv_ref, att_ref,
):
    rows, width = tokens_ref.shape
    me = lax.axis_index("unit")
    peers = counts_ref.shape[0]
    out_slots = cot_ref.shape[0] // 4
    factor = HEAD_DIM ** (-0.5)
    blocks = rows // BLK

    before = jnp.zeros((8, LANES), jnp.int32)
    for k in range(peers):
        before = before + jnp.where(k < me, counts_ref[k], 0)
    shift = before[0:1, :] - me * out_slots
    live = live_ref[0, 0]

    x = tokens_ref[...].astype(F32)
    n_one, p_one = normalize(x)
    n_one_ref[...] = n_one
    normed = (n_one * gain_one_ref[...]).astype(BF)
    qkv_ref[...] = nn(normed, w_qkv_ref[...]).astype(BF)

    same = (
        lax.broadcasted_iota(jnp.int32, (HEADS * BLK, BLK), 0) & (BLK - 1)
    ) >> 4 == lax.broadcasted_iota(jnp.int32, (HEADS * BLK, BLK), 1) >> 4
    for b in range(blocks):
        span = slice(b * BLK, (b + 1) * BLK)
        query = head_rows(qkv_ref[span, :width])
        scores = nt(query, qkv_ref[span, width : 2 * width]) * factor
        scores = jnp.where(same, scores, -1e30)
        e = jnp.exp(scores - jnp.max(scores, axis=-1, keepdims=True))
        att = e * (1.0 / jnp.sum(e, axis=-1, keepdims=True))
        att_ref[b] = att
        value = head_rows(qkv_ref[span, 2 * width :])
        mixed_ref[span, :] = nn(heads_to_lanes(att.astype(BF)), value).astype(BF)

    n_two, p_two = normalize(x + nn(mixed_ref[...], w_out_ref[...]))
    n_two_ref[...] = n_two
    y = n_two * gain_two_ref[...]
    high = y.astype(BF)
    low = (y - high.astype(F32)).astype(BF)
    ranked = 2 * 4 * out_slots
    gather = selection((ranked, rows), 1, before[0:1, 0:1] - me * out_slots, live)
    spread = selection((rows, ranked), 0, shift[:, :ranked], live)
    grouped = (nn(gather, high) + nn(gather, low)).astype(BF)
    pooled_ref[...] = nn(grouped, w_pool_ref[...]).astype(BF)

    cots = jnp.concatenate([cot_ref[...], next_ref[...]], axis=0)
    grad_pool = tn(grouped, cots).astype(BF)
    g_scaled = nt(nn(spread, cots).astype(BF), w_pool_ref[...])
    n_two = n_two_ref[...]
    g_ref[2016:2048, :] = gain_rows(jnp.sum(g_scaled * n_two, axis=0, keepdims=True))
    g_resid = norm_back(g_scaled * gain_two_ref[...], n_two, p_two)
    gr_ref[...] = g_resid
    resid_b = g_resid.astype(BF)
    grad_out = tn(mixed_ref[...], resid_b).astype(BF)
    for k in range(4):
        g_ref[width * k : width * (k + 1), :] = grad_pool[:, LANES * k : LANES * (k + 1)]
    g_ref[width * 4 : width * 5, :] = jnp.concatenate(
        [grad_pool[:, 512:576], grad_out[:, 256:288], jnp.zeros((width, 32), BF)], axis=1
    )
    g_ref[width * 5 : width * 6, :] = grad_out[:, :128]
    g_ref[width * 6 : width * 7, :] = grad_out[:, 128:256]

    mixed_ref[...] = nt(resid_b, w_out_ref[...]).astype(BF)
    for b in range(blocks):
        span = slice(b * BLK, (b + 1) * BLK)
        att = att_ref[b]
        g_mixed = head_rows(mixed_ref[span, :])
        g_att = nt(g_mixed, qkv_ref[span, 2 * width :])
        g_value = tn(att.astype(BF), g_mixed).astype(BF)
        g_scores = (att * (g_att - jnp.sum(g_att * att, axis=-1, keepdims=True)) * factor).astype(BF)
        g_query = nn(heads_to_lanes(g_scores), head_rows(qkv_ref[span, width : 2 * width])).astype(BF)
        g_key = tn(g_scores, head_rows(qkv_ref[span, :width])).astype(BF)
        gqkv_ref[span, :] = jnp.concatenate([g_query, g_key, g_value], axis=1)

    g_qkv = gqkv_ref[...]
    n_one = n_one_ref[...]
    normed = (n_one * gain_one_ref[...]).astype(BF)
    grad_qkv = tn(normed, g_qkv).astype(BF)
    for k in range(6):
        g_ref[HALF + width * k : HALF + width * (k + 1), :] = grad_qkv[:, LANES * k : LANES * (k + 1)]
    g_ref[HALF + width * 6 : HALF + width * 7, :] = jnp.concatenate(
        [grad_qkv[:, 768:864], jnp.zeros((width, 32), BF)], axis=1
    )
    g_normed = nt(g_qkv, w_qkv_ref[...])
    g_ref[HALF + 2016 : HALF + 2048, :] = gain_rows(jnp.sum(g_normed * n_one, axis=0, keepdims=True))
    g_input = norm_back(g_normed * gain_one_ref[...], n_one, p_one)
    grad_tokens_ref[...] = (gr_ref[...] + g_input).astype(BF)


def exchange_kernel(live_ref, cot_ref, counts_ref, next_ref, send_sem, count_sem, cot_sems):
    me = lax.axis_index("unit")
    peers = counts_ref.shape[0]
    barrier = pltpu.get_barrier_semaphore()
    for d in range(1, peers):
        pl.semaphore_signal(barrier, inc=1, device_id={"unit": lax.rem(me + d, peers)}, device_id_type=MESH)
    counts_ref[me] = jnp.full((8, LANES), live_ref[0, 0], jnp.int32)
    pl.semaphore_wait(barrier, peers - 1)
    shift = pltpu.make_async_remote_copy(
        src_ref=cot_ref, dst_ref=next_ref, send_sem=cot_sems.at[0], recv_sem=cot_sems.at[1],
        device_id={"unit": lax.rem(me + peers - 1, peers)}, device_id_type=MESH,
    )
    shift.start()
    for d in range(1, peers):
        pltpu.make_async_remote_copy(
            src_ref=counts_ref.at[me], dst_ref=counts_ref.at[me], send_sem=send_sem, recv_sem=count_sem,
            device_id={"unit": lax.rem(me + d, peers)}, device_id_type=MESH,
        ).start()
    others = counts_ref.at[pl.ds(0, peers - 1)]
    pltpu.make_async_copy(others, others, send_sem).wait()
    pltpu.make_async_copy(others, others, count_sem).wait()
    shift.wait()


def reduce_kernel(
    g_ref, pooled_ref, f_ref, prev_ref, r_one, s_ref, r_two, t_ref, r_three, w_ref, u_ref,
    pool_sems, one_send, one_recv, two_send, two_recv, three_send, three_recv, four_send, four_recv,
    five_send, five_recv, six_send, six_recv,
):
    me = lax.axis_index("unit")
    z = lax.axis_index("img")
    units = lax.axis_size("unit")
    nz = lax.axis_size("img")
    chips = units // 2
    core = lax.rem(me, 2)
    chip = me // 2
    half = HALF // 2
    piece = half // chips
    owners = nz // 2
    tile = 2 * piece // owners
    sibling = me + 1 - 2 * core
    other = lax.rem(me + units + 2 * core - 1, units)

    def plane(d):
        return lax.rem(chip + d, chips) * 2 + core

    barrier = pltpu.get_barrier_semaphore()
    pl.semaphore_signal(barrier, inc=1, device_id={"unit": sibling}, device_id_type=MESH)
    pl.semaphore_signal(barrier, inc=1, device_id={"unit": other}, device_id_type=MESH)
    for d in range(1, chips):
        pl.semaphore_signal(barrier, inc=1, device_id={"unit": plane(d)}, device_id_type=MESH)
    for d in range(1, nz):
        pl.semaphore_signal(barrier, inc=1, device_id={"img": lax.rem(z + d, nz)}, device_id_type=MESH)
    pl.semaphore_wait(barrier, chips + nz)

    firsts = []
    for part in range(2):
        copy = pltpu.make_async_remote_copy(
            src_ref=g_ref.at[pl.ds(pl.multiple_of(part * HALF + (1 - core) * half, half), half)],
            dst_ref=r_one.at[part], send_sem=one_send.at[part], recv_sem=one_recv.at[part],
            device_id={"unit": sibling}, device_id_type=MESH,
        )
        copy.start()
        firsts.append(copy)
    pooled_copy = pltpu.make_async_remote_copy(
        src_ref=pooled_ref.at[pl.ds(pooled_ref.shape[0] // 2, pooled_ref.shape[0] // 2)], dst_ref=prev_ref,
        send_sem=pool_sems.at[0], recv_sem=pool_sems.at[1],
        device_id={"unit": lax.rem(me + 1, units)}, device_id_type=MESH,
    )
    pooled_copy.start()

    for part in range(2):
        firsts[part].wait_recv()
        own = g_ref[pl.ds(pl.multiple_of(part * HALF + core * half, half), half), :]
        s_ref[part] = (own.astype(F32) + r_one[part].astype(F32)).astype(BF)
        for d in range(1, chips):
            pltpu.make_async_remote_copy(
                src_ref=s_ref.at[part, pl.ds(pl.multiple_of(lax.rem(chip + d, chips) * piece, piece), piece)],
                dst_ref=r_two.at[part, d], send_sem=two_send.at[part], recv_sem=two_recv.at[part],
                device_id={"unit": plane(d)}, device_id_type=MESH,
            ).start()
    for part in range(2):
        landed = r_two.at[part, pl.ds(1, chips - 1)]
        pltpu.make_async_copy(landed, landed, two_recv.at[part]).wait()
        total = s_ref[part, pl.ds(pl.multiple_of(chip * piece, piece), piece), :].astype(F32)
        for d in range(1, chips):
            total = total + r_two[part, d].astype(F32)
        t_ref[pl.ds(part * piece, piece), :] = total.astype(BF)

    for t in range(owners):
        owner = lax.rem(2 * t + core, nz)

        @pl.when(owner != z)
        def _():
            pltpu.make_async_remote_copy(
                src_ref=t_ref.at[pl.ds(t * tile, tile)], dst_ref=r_three.at[z], send_sem=three_send,
                recv_sem=three_recv, device_id={"img": owner}, device_id_type=MESH,
            ).start()

    owning = lax.rem(z, 2) == core
    mine = (z - lax.rem(z, 2)) // 2
    span = pl.ds(pl.multiple_of(mine * tile, tile), tile)

    @pl.when(owning)
    def _():
        r_three[z] = t_ref[span, :]
        landed = r_three.at[pl.ds(0, nz - 1)]
        pltpu.make_async_copy(landed, landed, three_recv).wait()
        total = r_three[0].astype(F32)
        for k in range(1, nz):
            total = total + r_three[k].astype(F32)
        u_ref[...] = total.astype(BF)
        for d in range(1, nz):
            pltpu.make_async_remote_copy(
                src_ref=u_ref, dst_ref=w_ref.at[span], send_sem=four_send,
                recv_sem=four_recv, device_id={"img": lax.rem(z + d, nz)}, device_id_type=MESH,
            ).start()
        w_ref[span, :] = u_ref[...]
        if owners > 1:
            rest = w_ref.at[pl.ds(0, (owners - 1) * tile)]
            pltpu.make_async_copy(rest, rest, four_recv).wait()
            pltpu.make_async_copy(rest, rest, three_send).wait()
        sent = r_three.at[pl.ds(0, nz - 1)]
        pltpu.make_async_copy(sent, sent, four_send).wait()

    @pl.when(jnp.logical_not(owning))
    def _():
        pltpu.make_async_copy(w_ref, w_ref, four_recv).wait()
        pltpu.make_async_copy(w_ref, w_ref, three_send).wait()

    chunk = 2 * piece

    def place(which_core, which_chip):
        return pl.ds(pl.multiple_of(which_core * HALF + which_chip * chunk, chunk), chunk)

    for d in range(1, chips):
        pltpu.make_async_remote_copy(
            src_ref=w_ref, dst_ref=f_ref.at[place(core, chip)], send_sem=five_send,
            recv_sem=five_recv.at[d], device_id={"unit": plane(d)}, device_id_type=MESH,
        ).start()
    f_ref[place(core, chip), :] = w_ref[...]
    for d in range(chips):
        source = lax.rem(chip + chips - d, chips)
        if d > 0:
            arrived = f_ref.at[place(core, source)]
            pltpu.make_async_copy(arrived, arrived, five_recv.at[d]).wait()
        pltpu.make_async_remote_copy(
            src_ref=f_ref.at[place(core, source)], dst_ref=f_ref.at[place(core, source)],
            send_sem=six_send, recv_sem=six_recv, device_id={"unit": sibling}, device_id_type=MESH,
        ).start()
    whole = f_ref.at[pl.ds(0, HALF)]
    pltpu.make_async_copy(whole, whole, six_send).wait()
    pltpu.make_async_copy(whole, whole, six_recv).wait()
    sent = f_ref.at[pl.ds(0, (chips - 1) * chunk)]
    pltpu.make_async_copy(sent, sent, five_send).wait()
    for part in range(2):
        firsts[part].wait_send()
        sent = s_ref.at[part, pl.ds(0, (chips - 1) * piece)]
        pltpu.make_async_copy(sent, sent, two_send.at[part]).wait()
    pooled_copy.wait()


def unpack_kernel(chips, scale, f_ref, pooled_ref, prev_ref, out_ref, qkv_ref, go_ref, pool_ref, one_ref, two_ref):
    piece = HALF // 2 // chips
    chunk = 2 * piece
    width = go_ref.shape[0]
    step = 32

    def rows32(part, row):
        half = HALF // 2
        core, rest = row // half, row % half
        at = core * HALF + rest // piece * chunk + part * piece + rest % piece
        return f_ref[at : at + step, :].astype(F32) * scale

    for k in range(7):
        for r in range(0, width, step):
            span = slice(r, r + step)
            early = rows32(0, width * k + r)
            late = rows32(1, width * k + r)
            if k < 6:
                qkv_ref[span, LANES * k : LANES * (k + 1)] = late
            else:
                qkv_ref[span, 768:864] = late[:, :96]
            if k < 4:
                pool_ref[span, LANES * k : LANES * (k + 1)] = early
            elif k == 4:
                pool_ref[span, 512:576] = early[:, :64]
                go_ref[span, 256:288] = early[:, 64:96]
            else:
                go_ref[span, LANES * (k - 5) : LANES * (k - 4)] = early
    for part, ref in ((0, two_ref), (1, one_ref)):
        last = rows32(part, 2016)
        ref[...] = jnp.concatenate([last[0:1], last[1:2], last[2:3, :32]], axis=1)
    own = pooled_ref[: out_ref.shape[0], :]
    out_ref[...] = own + prev_ref[...]


def full(count):
    return [pl.BlockSpec(memory_space=pltpu.VMEM)] * count


def local(tokens, live, cotangent, w_qkv, w_out, w_pool, gain_one, gain_two):
    img_dev, slots, token_count, width = tokens.shape
    out_slots, out_width = cotangent.shape[1], cotangent.shape[3]
    units, nz = lax.axis_size("unit"), lax.axis_size("img")
    chips = units // 2
    rows = slots * token_count
    crows = out_slots * 4
    piece = HALF // 2 // chips
    tile = 2 * piece // (nz // 2)
    cot = cotangent.reshape(crows, out_width)
    tok = tokens.reshape(rows, width)
    dma, smem = pltpu.SemaphoreType.DMA, pl.BlockSpec(memory_space=pltpu.SMEM)

    def sd(shape, dtype):
        return jax.ShapeDtypeStruct(shape, dtype)

    counts, next_cot = pl.pallas_call(
        exchange_kernel,
        out_shape=(sd((units, 8, LANES), jnp.int32), sd((crows, out_width), BF)),
        in_specs=[smem] + full(1),
        out_specs=full(2),
        scratch_shapes=[dma, dma, dma((2,))],
        compiler_params=pltpu.CompilerParams(collective_id=0, has_side_effects=True, vmem_limit_bytes=VMEM_LIMIT),
        name="exchange",
    )(live, cot)

    grad_tokens, pooled, g = pl.pallas_call(
        compute_kernel,
        out_shape=(sd((rows, width), BF), sd((2 * crows, out_width), BF), sd((2 * HALF, LANES), BF)),
        in_specs=[smem] + full(9),
        out_specs=full(3),
        scratch_shapes=[
            pltpu.VMEM((rows, width), F32),
            pltpu.VMEM((rows, width), F32),
            pltpu.VMEM((rows, width), F32),
            pltpu.VMEM((rows, 3 * width), BF),
            pltpu.VMEM((rows, width), BF),
            pltpu.VMEM((rows, 3 * width), BF),
            pltpu.VMEM((rows // BLK, HEADS * BLK, BLK), F32),
        ],
        compiler_params=pltpu.CompilerParams(vmem_limit_bytes=VMEM_LIMIT),
        name="compute",
    )(live, counts, tok, cot, next_cot, w_qkv, w_out, w_pool, gain_one[None], gain_two[None])

    f, prev = pl.pallas_call(
        reduce_kernel,
        out_shape=(sd((2 * HALF, LANES), BF), sd((crows, out_width), BF)),
        in_specs=full(2),
        out_specs=full(2),
        scratch_shapes=[
            pltpu.VMEM((2, HALF // 2, LANES), BF),
            pltpu.VMEM((2, HALF // 2, LANES), BF),
            pltpu.VMEM((2, chips, piece, LANES), BF),
            pltpu.VMEM((2 * piece, LANES), BF),
            pltpu.VMEM((nz, tile, LANES), BF),
            pltpu.VMEM((2 * piece, LANES), BF),
            pltpu.VMEM((tile, LANES), BF),
            dma((2,)), dma((2,)), dma((2,)), dma((2,)), dma((2,)), dma, dma, dma, dma,
            dma, dma((chips,)), dma, dma,
        ],
        compiler_params=pltpu.CompilerParams(collective_id=1, has_side_effects=True, vmem_limit_bytes=VMEM_LIMIT),
        name="reduce",
    )(g, pooled)

    scale = 1.0 / math.sqrt(img_dev * nz * out_slots * units)
    out, grad_qkv, grad_out, grad_pool, one, two = pl.pallas_call(
        functools.partial(unpack_kernel, chips, scale),
        out_shape=(
            sd((crows, out_width), BF), sd((width, 3 * width), F32), sd((width, width), F32),
            sd((width, out_width), F32), sd((1, width), F32), sd((1, width), F32),
        ),
        in_specs=full(3),
        out_specs=full(6),
        compiler_params=pltpu.CompilerParams(vmem_limit_bytes=VMEM_LIMIT),
        name="unpack",
    )(f, pooled, prev)
    return (
        out.reshape(cotangent.shape), grad_tokens.reshape(tokens.shape),
        grad_qkv, grad_out, grad_pool, one.reshape(width), two.reshape(width),
    )


def solution(mesh):
    return jax.shard_map(
        local,
        mesh=mesh,
        in_specs=(
            P("img", "unit", None, None), P("img", "unit"), P("img", "unit", None, None),
            P(), P(), P(), P(), P(),
        ),
        out_specs=(P("img", "unit", None, None), P("img", "unit", None, None), P(), P(), P(), P(), P()),
        check_vma=False,
    )
```

```python
import functools
import math

import jax
import jax.numpy as jnp
from jax import lax
from jax.experimental import pallas as pl
from jax.experimental.pallas import tpu as pltpu
from jax.sharding import PartitionSpec as P

HEADS = 4
HEAD_DIM = 72
EPSILON = 1e-06
BF = jnp.bfloat16
F32 = jnp.float32
MESH = pl.DeviceIdType.MESH
TOK = 16
BLK = 128
LANES = 128
HALF = 2048
AROUND = {1: (0,), 2: (1, 0), 4: (2, 1, 3, 0)}
VMEM_LIMIT = 62 * 1024 * 1024


def nn(a, b):
    return lax.dot_general(a, b, (((1,), (0,)), ((), ())), preferred_element_type=F32)


def nt(a, b):
    return lax.dot_general(a, b, (((1,), (1,)), ((), ())), preferred_element_type=F32)


def tn(a, b):
    return lax.dot_general(a, b, (((0,), (0,)), ((), ())), preferred_element_type=F32)


def normalize(values):
    centred = values - jnp.mean(values, axis=-1, keepdims=True)
    inv_scale = lax.rsqrt(jnp.mean(centred * centred, axis=-1, keepdims=True) + EPSILON)
    return centred * inv_scale, inv_scale


def norm_back(grad_norm, normed_v, inv_scale):
    first = jnp.mean(grad_norm, axis=-1, keepdims=True)
    second = jnp.mean(grad_norm * normed_v, axis=-1, keepdims=True)
    return inv_scale * (grad_norm - first - normed_v * second)


def selection(shape, token_dim, shift, live):
    token = lax.broadcasted_iota(jnp.int32, shape, token_dim)
    row = lax.broadcasted_iota(jnp.int32, shape, 1 - token_dim)
    slot = token >> 4
    group = ((token >> 3) & 1) * 2 + ((token >> 1) & 1)
    hit = (row == (shift + slot) * 4 + group) & (slot < live)
    return jnp.where(hit, 0.25, 0.0).astype(BF)


def head_rows(block):
    lane = lax.broadcasted_iota(jnp.int32, (1, block.shape[1]), 1)
    parts = []
    for head in range(HEADS):
        mine = (lane >= head * HEAD_DIM) & (lane < (head + 1) * HEAD_DIM)
        parts.append(block * jnp.where(mine, 1.0, 0.0).astype(BF))
    return jnp.concatenate(parts, axis=0)


def heads_to_lanes(rows):
    return jnp.concatenate([rows[h * BLK : (h + 1) * BLK] for h in range(HEADS)], axis=1)


def gain_rows(total):
    row = lax.broadcasted_iota(jnp.int32, (32, LANES), 0)
    last = jnp.concatenate([total[:, 256:], jnp.zeros((1, 96), F32)], axis=1)
    out = jnp.where(row == 0, total[:, :128], 0.0)
    out = jnp.where(row == 1, total[:, 128:256], out)
    return jnp.where(row == 2, last, out).astype(BF)


def main_kernel(
    live_ref, tok_hbm, cot_hbm, w_qkv_hbm, w_out_hbm, w_pool_hbm, gain_one_hbm, gain_two_hbm,
    f_ref, pooled_out, grad_tokens_ref,
    tok_ref, cot_ref, w_qkv_ref, w_out_ref, w_pool_ref, gain_one_ref, gain_two_ref,
    counts_ref, cots_ref, pooled_ref, prev_ref, g_ref, n_one_ref, n_two_ref, gr_ref, qkv_ref, mixed_ref, gqkv_ref,
    att_ref, r_one, s_ref, r_two, t_ref, r_three, u_ref, w_ref,
    in_sems, count_sems, cot_sems, pool_sems, one_send, one_recv, two_send, two_recv, three_send, three_recv,
    four_send, four_recv, five_send, five_recv, six_send, six_recv,
):
    rows, width = tok_ref.shape
    crows = cots_ref.shape[0] // 2
    out_slots = crows // 4
    factor = HEAD_DIM ** (-0.5)
    blocks = rows // BLK
    me = lax.axis_index("unit")
    z = lax.axis_index("img")
    units = lax.axis_size("unit")
    nz = lax.axis_size("img")
    chips = units // 2
    nx = min(4, chips)
    ny = chips // nx
    core = lax.rem(me, 2)
    chip = me // 2
    chip_x, chip_y = lax.rem(chip, nx), chip // nx
    half = HALF // 2
    piece = half // chips
    tile = piece // 4
    sibling = me + 1 - 2 * core
    plane = [(dx, dy) for dx in AROUND[nx] for dy in AROUND[ny]][:-1]

    def chip_at(dx, dy):
        return lax.rem(chip_y + dy, ny) * nx + lax.rem(chip_x + dx, nx)

    def fetch(k, source, target):
        copy = pltpu.make_async_copy(source, target, in_sems.at[k])
        copy.start()
        return copy

    def push(source, target, send, recv, **where):
        copy = pltpu.make_async_remote_copy(
            src_ref=source, dst_ref=target, send_sem=send, recv_sem=recv, device_id=where, device_id_type=MESH
        )
        copy.start()
        return copy

    def drain(ref, sem):
        pltpu.make_async_copy(ref, ref, sem).wait()

    get_tok = fetch(0, tok_hbm, tok_ref)
    get_gain_one = fetch(1, gain_one_hbm, gain_one_ref)
    get_w_qkv = fetch(2, w_qkv_hbm, w_qkv_ref)
    get_cot = fetch(3, cot_hbm, cot_ref)
    get_w_out = fetch(4, w_out_hbm, w_out_ref)
    get_gain_two = fetch(5, gain_two_hbm, gain_two_ref)
    get_w_pool = fetch(6, w_pool_hbm, w_pool_ref)

    barrier = pltpu.get_barrier_semaphore()
    for d in range(1, nz):
        pl.semaphore_signal(barrier, inc=1, device_id={"img": lax.rem(z + d, nz)}, device_id_type=MESH)
    for d in range(1, units):
        pl.semaphore_signal(barrier, inc=1, device_id={"unit": lax.rem(me + d, units)}, device_id_type=MESH)

    def half_of(part, which):
        return pl.ds(pl.multiple_of(part * HALF + which * half, half), half)

    def pair_send(part):
        push(g_ref.at[half_of(part, 1 - core)], r_one.at[part], one_send.at[part], one_recv.at[part], unit=sibling)

    def pair_add(part):
        drain(r_one.at[part], one_recv.at[part])
        own = g_ref[half_of(part, core), :]
        s_ref[part] = (own.astype(F32) + r_one[part].astype(F32)).astype(BF)
        for k, (dx, dy) in enumerate(plane):
            there = chip_at(dx, dy)
            push(
                s_ref.at[part, pl.ds(pl.multiple_of(there * piece, piece), piece)], r_two.at[part, k],
                two_send.at[part], two_recv.at[part], unit=there * 2 + core,
            )

    def plane_add(part):
        drain(r_two.at[part], two_recv.at[part])
        total = s_ref[part, pl.ds(pl.multiple_of(chip * piece, piece), piece), :].astype(F32)
        for k in range(chips - 1):
            total = total + r_two[part, k].astype(F32)
        t_ref[part] = total.astype(BF)
        for d in range(1, nz):
            there = lax.rem(z + d, nz)
            push(
                t_ref.at[part, pl.ds(pl.multiple_of(lax.rem(there, 4) * tile, tile), tile)], r_three.at[part, z],
                three_send.at[part], three_recv.at[part], img=there,
            )
        r_three[part, z] = t_ref[part, pl.ds(pl.multiple_of(lax.rem(z, 4) * tile, tile), tile), :]

    mine = pl.ds(pl.multiple_of(lax.rem(z, 4) * tile, tile), tile)

    def line_add(part):
        drain(r_three.at[part, pl.ds(0, nz - 1)], three_recv.at[part])
        total = r_three[part, 0].astype(F32)
        for k in range(1, nz):
            total = total + r_three[part, k].astype(F32)
        u_ref[part] = total.astype(BF)
        for d in (2, 1, nz - 1):
            push(u_ref.at[part], w_ref.at[part, mine], four_send.at[part], four_recv.at[part], img=lax.rem(z + d, nz))
        w_ref[part, mine, :] = u_ref[part]

    def place(part, which_core, which_chip):
        return pl.ds(pl.multiple_of(part * HALF + which_core * half + which_chip * piece, piece), piece)

    def plane_spread(part):
        drain(w_ref.at[part, pl.ds(0, 3 * tile)], four_recv.at[part])
        here = place(part, core, chip)
        for k, (dx, dy) in enumerate(plane):
            push(
                w_ref.at[part], f_ref.at[here], five_send.at[part], five_recv.at[part, k],
                unit=chip_at(dx, dy) * 2 + core,
            )
        f_ref[here, :] = w_ref[part]
        push(w_ref.at[part], f_ref.at[here], six_send.at[part], six_recv.at[part], unit=sibling)

    def pair_spread(part):
        for k, (dx, dy) in reversed(list(enumerate(plane))):
            there = place(part, core, chip_at(nx - dx, ny - dy))
            drain(f_ref.at[there], five_recv.at[part, k])
            push(f_ref.at[there], f_ref.at[there], six_send.at[part], six_recv.at[part], unit=sibling)

    get_tok.wait()
    get_gain_one.wait()
    n_one, p_one = normalize(tok_ref[...].astype(F32))
    n_one_ref[...] = n_one
    normed = (n_one * gain_one_ref[...]).astype(BF)
    get_w_qkv.wait()
    qkv_ref[...] = nn(normed, w_qkv_ref[...]).astype(BF)

    same = (
        lax.broadcasted_iota(jnp.int32, (HEADS * BLK, BLK), 0) & (BLK - 1)
    ) >> 4 == lax.broadcasted_iota(jnp.int32, (HEADS * BLK, BLK), 1) >> 4
    for b in range(blocks):
        span = slice(b * BLK, (b + 1) * BLK)
        query = head_rows(qkv_ref[span, :width])
        scores = nt(query, qkv_ref[span, width : 2 * width]) * factor
        scores = jnp.where(same, scores, -1e30)
        e = jnp.exp(scores - jnp.max(scores, axis=-1, keepdims=True))
        att = e * (1.0 / jnp.sum(e, axis=-1, keepdims=True))
        att_ref[b] = att
        value = head_rows(qkv_ref[span, 2 * width :])
        mixed_ref[span, :] = nn(heads_to_lanes(att.astype(BF)), value).astype(BF)

    get_cot.wait()
    cots_ref[:crows, :] = cot_ref[...].reshape(crows, cots_ref.shape[1])
    counts_ref[me] = jnp.full((8, LANES), live_ref[0, 0], jnp.int32)
    pl.semaphore_wait(barrier, nz + units - 2)
    for d in range(1, units):
        push(counts_ref.at[me], counts_ref.at[me], count_sems.at[0], count_sems.at[1], unit=lax.rem(me + d, units))
    cot_copy = push(
        cots_ref.at[pl.ds(0, crows)], cots_ref.at[pl.ds(crows, crows)], cot_sems.at[0], cot_sems.at[1],
        unit=lax.rem(me + units - 1, units),
    )

    get_w_out.wait()
    get_gain_two.wait()
    n_two, p_two = normalize(tok_ref[...].astype(F32) + nn(mixed_ref[...], w_out_ref[...]))
    n_two_ref[...] = n_two
    y = n_two * gain_two_ref[...]
    high = y.astype(BF)
    low = (y - high.astype(F32)).astype(BF)

    get_w_pool.wait()
    others = counts_ref.at[pl.ds(0, units - 1)]
    drain(others, count_sems.at[1])
    before = jnp.zeros((8, LANES), jnp.int32)
    for k in range(units):
        before = before + jnp.where(k < me, counts_ref[k], 0)
    shift = before[0:1, :] - me * out_slots
    live = live_ref[0, 0]
    ranked = 2 * crows
    gather = selection((ranked, rows), 1, shift[:, 0:1], live)
    spread = selection((rows, ranked), 0, shift[:, :ranked], live)
    grouped = (nn(gather, high) + nn(gather, low)).astype(BF)
    pooled_ref[...] = nn(grouped, w_pool_ref[...]).astype(BF)
    pooled_copy = push(
        pooled_ref.at[pl.ds(crows, crows)], prev_ref, pool_sems.at[0], pool_sems.at[1],
        unit=lax.rem(me + 1, units),
    )

    cot_copy.wait_recv()
    cots = cots_ref[...]
    grad_pool = tn(grouped, cots).astype(BF)
    g_scaled = nt(nn(spread, cots).astype(BF), w_pool_ref[...])
    n_two = n_two_ref[...]
    g_ref[2016:2048, :] = gain_rows(jnp.sum(g_scaled * n_two, axis=0, keepdims=True))
    g_resid = norm_back(g_scaled * gain_two_ref[...], n_two, p_two)
    gr_ref[...] = g_resid
    resid_b = g_resid.astype(BF)
    grad_out = tn(mixed_ref[...], resid_b).astype(BF)
    for k in range(4):
        g_ref[width * k : width * (k + 1), :] = grad_pool[:, LANES * k : LANES * (k + 1)]
    g_ref[width * 4 : width * 5, :] = jnp.concatenate(
        [grad_pool[:, 512:576], grad_out[:, 256:288], jnp.zeros((width, 32), BF)], axis=1
    )
    g_ref[width * 5 : width * 6, :] = grad_out[:, :128]
    g_ref[width * 6 : width * 7, :] = grad_out[:, 128:256]
    pair_send(0)

    mixed_ref[...] = nt(resid_b, w_out_ref[...]).astype(BF)
    for b in range(blocks):
        span = slice(b * BLK, (b + 1) * BLK)
        att = att_ref[b]
        g_mixed = head_rows(mixed_ref[span, :])
        g_att = nt(g_mixed, qkv_ref[span, 2 * width :])
        g_value = tn(att.astype(BF), g_mixed).astype(BF)
        g_scores = (att * (g_att - jnp.sum(g_att * att, axis=-1, keepdims=True)) * factor).astype(BF)
        g_query = nn(heads_to_lanes(g_scores), head_rows(qkv_ref[span, width : 2 * width])).astype(BF)
        g_key = tn(g_scores, head_rows(qkv_ref[span, :width])).astype(BF)
        gqkv_ref[span, :] = jnp.concatenate([g_query, g_key, g_value], axis=1)
        if b == blocks - 2:
            pair_add(0)

    g_qkv = gqkv_ref[...]
    n_one = n_one_ref[...]
    normed = (n_one * gain_one_ref[...]).astype(BF)
    grad_qkv = tn(normed, g_qkv).astype(BF)
    for k in range(6):
        g_ref[HALF + width * k : HALF + width * (k + 1), :] = grad_qkv[:, LANES * k : LANES * (k + 1)]
    g_ref[HALF + width * 6 : HALF + width * 7, :] = jnp.concatenate(
        [grad_qkv[:, 768:864], jnp.zeros((width, 32), BF)], axis=1
    )
    g_normed = nt(g_qkv, w_qkv_ref[...])
    g_ref[HALF + 2016 : HALF + 2048, :] = gain_rows(jnp.sum(g_normed * n_one, axis=0, keepdims=True))
    pair_send(1)
    g_input = norm_back(g_normed * gain_one_ref[...], n_one, p_one)
    grad_tokens_ref[...] = (gr_ref[...] + g_input).astype(BF)

    pair_add(1)
    plane_add(0)
    pooled_copy.wait_recv()
    pooled_out[...] = pooled_ref[:crows, :] + prev_ref[...]
    plane_add(1)
    line_add(0)
    plane_spread(0)
    line_add(1)
    plane_spread(1)
    pair_spread(0)
    pair_spread(1)

    for part in range(2):
        drain(g_ref.at[pl.ds(0, half)], one_send.at[part])
        drain(r_two.at[part], two_send.at[part])
        drain(r_three.at[part, pl.ds(0, nz - 1)], three_send.at[part])
        drain(w_ref.at[part, pl.ds(0, 3 * tile)], four_send.at[part])
        drain(f_ref.at[pl.ds(0, half - piece)], five_send.at[part])
        drain(f_ref.at[pl.ds(0, half)], six_send.at[part])
        drain(f_ref.at[pl.ds(0, half)], six_recv.at[part])
    drain(others, count_sems.at[0])
    cot_copy.wait_send()
    pooled_copy.wait_send()


def unpack_kernel(
    scale, f_ref, pooled_ref, tok_ref, out_ref, grad_tokens_ref, qkv_ref, go_ref, pool_ref, one_ref, two_ref
):
    width = go_ref.shape[0]

    def rows(start, count):
        return f_ref[start : start + count, :].astype(F32) * scale

    for k in range(7):
        early = rows(width * k, width)
        late = rows(HALF + width * k, width)
        if k < 6:
            qkv_ref[:, LANES * k : LANES * (k + 1)] = late
        else:
            qkv_ref[:, 768:864] = late[:, :96]
        if k < 4:
            pool_ref[:, LANES * k : LANES * (k + 1)] = early
        elif k == 4:
            pool_ref[:, 512:576] = early[:, :64]
            go_ref[:, 256:288] = early[:, 64:96]
        else:
            go_ref[:, LANES * (k - 5) : LANES * (k - 4)] = early
    for start, ref in ((2016, two_ref), (HALF + 2016, one_ref)):
        last = rows(start, 32)
        ref[...] = jnp.concatenate([last[0:1], last[1:2], last[2:3, :32]], axis=1).reshape(ref.shape)
    out_ref[...] = pooled_ref[...].reshape(out_ref.shape)
    grad_tokens_ref[...] = tok_ref[...]


def whole(count, space=pltpu.VMEM):
    return [pl.BlockSpec(memory_space=space)] * count


def local(tokens, live, cotangent, w_qkv, w_out, w_pool, gain_one, gain_two):
    img_dev, slots, token_count, width = tokens.shape
    out_slots, out_width = cotangent.shape[1], cotangent.shape[3]
    units, nz = lax.axis_size("unit"), lax.axis_size("img")
    chips = units // 2
    rows = slots * token_count
    crows = out_slots * 4
    piece = HALF // 2 // chips
    dma, vmem = pltpu.SemaphoreType.DMA, pltpu.VMEM

    def sd(shape, dtype):
        return jax.ShapeDtypeStruct(shape, dtype)

    f, pooled, grad_tok = pl.pallas_call(
        main_kernel,
        out_shape=(sd((2 * HALF, LANES), BF), sd((crows, out_width), BF), sd((rows, width), BF)),
        in_specs=[pl.BlockSpec(memory_space=pltpu.SMEM)] + whole(7, pltpu.HBM),
        out_specs=whole(3),
        scratch_shapes=[
            vmem((rows, width), BF),
            vmem((out_slots, 4, out_width), BF),
            vmem(w_qkv.shape, BF),
            vmem(w_out.shape, BF),
            vmem(w_pool.shape, BF),
            vmem(gain_one.shape, F32),
            vmem(gain_two.shape, F32),
            vmem((units, 8, LANES), jnp.int32),
            vmem((2 * crows, out_width), BF),
            vmem((2 * crows, out_width), BF),
            vmem((crows, out_width), BF),
            vmem((2 * HALF, LANES), BF),
            vmem((rows, width), F32),
            vmem((rows, width), F32),
            vmem((rows, width), F32),
            vmem((rows, 3 * width), BF),
            vmem((rows, width), BF),
            vmem((rows, 3 * width), BF),
            vmem((rows // BLK, HEADS * BLK, BLK), F32),
            vmem((2, HALF // 2, LANES), BF),
            vmem((2, HALF // 2, LANES), BF),
            vmem((2, chips - 1, piece, LANES), BF),
            vmem((2, piece, LANES), BF),
            vmem((2, nz, piece // 4, LANES), BF),
            vmem((2, piece // 4, LANES), BF),
            vmem((2, piece, LANES), BF),
            dma((7,)), dma((2,)), dma((2,)), dma((2,)), dma((2,)), dma((2,)), dma((2,)), dma((2,)), dma((2,)),
            dma((2,)), dma((2,)), dma((2,)), dma((2,)), dma((2, chips - 1)), dma((2,)), dma((2,)),
        ],
        compiler_params=pltpu.CompilerParams(collective_id=0, has_side_effects=True, vmem_limit_bytes=VMEM_LIMIT),
        name="main",
    )(
        live, tokens.reshape(rows, width), cotangent.reshape(out_slots, 4, out_width), w_qkv, w_out, w_pool,
        gain_one, gain_two,
    )

    scale = 1.0 / math.sqrt(img_dev * nz * out_slots * units)
    out, grad_tokens, grad_qkv, grad_out, grad_pool, one, two = pl.pallas_call(
        functools.partial(unpack_kernel, scale),
        out_shape=(
            sd((out_slots, 4, out_width), BF), sd((rows, width), BF), sd((width, 3 * width), F32),
            sd((width, width), F32), sd((width, out_width), F32), sd((width,), F32), sd((width,), F32),
        ),
        in_specs=whole(3),
        out_specs=whole(7),
        compiler_params=pltpu.CompilerParams(vmem_limit_bytes=VMEM_LIMIT),
        name="unpack",
    )(f, pooled, grad_tok)
    return (
        out.reshape(cotangent.shape), grad_tokens.reshape(tokens.shape), grad_qkv, grad_out, grad_pool, one, two,
    )


def solution(mesh):
    return jax.shard_map(
        local,
        mesh=mesh,
        in_specs=(
            P("img", "unit", None, None), P("img", "unit"), P("img", "unit", None, None),
            P(), P(), P(), P(), P(),
        ),
        out_specs=(P("img", "unit", None, None), P("img", "unit", None, None), P(), P(), P(), P(), P()),
        check_vma=False,
    )
```

```python
import functools
import math

import jax
import jax.numpy as jnp
from jax import lax
from jax.experimental import pallas as pl
from jax.experimental.pallas import tpu as pltpu
from jax.sharding import PartitionSpec as P

HEADS = 4
HEAD_DIM = 72
EPSILON = 1e-06
BF = jnp.bfloat16
F32 = jnp.float32
MESH = pl.DeviceIdType.MESH
TOK = 16
BLK = 128
LANES = 128
HALF = 2048
AROUND = {1: (0,), 2: (1, 0), 4: (2, 1, 3, 0)}
VMEM_LIMIT = 62 * 1024 * 1024
UNPACK_LIMIT = 24 * 1024 * 1024


def nn(a, b):
    return lax.dot_general(a, b, (((1,), (0,)), ((), ())), preferred_element_type=F32)


def nt(a, b):
    return lax.dot_general(a, b, (((1,), (1,)), ((), ())), preferred_element_type=F32)


def tn(a, b):
    return lax.dot_general(a, b, (((0,), (0,)), ((), ())), preferred_element_type=F32)


def normalize(values):
    centred = values - jnp.mean(values, axis=-1, keepdims=True)
    inv_scale = lax.rsqrt(jnp.mean(centred * centred, axis=-1, keepdims=True) + EPSILON)
    return centred * inv_scale, inv_scale


def norm_back(grad_norm, normed_v, inv_scale):
    first = jnp.mean(grad_norm, axis=-1, keepdims=True)
    second = jnp.mean(grad_norm * normed_v, axis=-1, keepdims=True)
    return inv_scale * (grad_norm - first - normed_v * second)


def selection(shape, token_dim, shift, live):
    token = lax.broadcasted_iota(jnp.int32, shape, token_dim)
    row = lax.broadcasted_iota(jnp.int32, shape, 1 - token_dim)
    slot = token >> 4
    group = ((token >> 3) & 1) * 2 + ((token >> 1) & 1)
    hit = (row == (shift + slot) * 4 + group) & (slot < live)
    return jnp.where(hit, 0.25, 0.0).astype(BF)


def head_rows(block):
    lane = lax.broadcasted_iota(jnp.int32, (1, block.shape[1]), 1)
    parts = []
    for head in range(HEADS):
        mine = (lane >= head * HEAD_DIM) & (lane < (head + 1) * HEAD_DIM)
        parts.append(block * jnp.where(mine, 1.0, 0.0).astype(BF))
    return jnp.concatenate(parts, axis=0)


def heads_to_lanes(rows):
    return jnp.concatenate([rows[h * BLK : (h + 1) * BLK] for h in range(HEADS)], axis=1)


def gain_rows(total):
    row = lax.broadcasted_iota(jnp.int32, (32, LANES), 0)
    last = jnp.concatenate([total[:, 256:], jnp.zeros((1, 96), F32)], axis=1)
    out = jnp.where(row == 0, total[:, :128], 0.0)
    out = jnp.where(row == 1, total[:, 128:256], out)
    return jnp.where(row == 2, last, out).astype(BF)


def main_kernel(
    live_ref, tok_hbm, cot_hbm, w_qkv_hbm, w_out_hbm, w_pool_hbm, gain_one_hbm, gain_two_hbm,
    f_ref, pooled_out, grad_tokens_ref,
    tok_ref, cot_ref, w_qkv_ref, w_out_ref, w_pool_ref, gain_one_ref, gain_two_ref,
    counts_ref, cots_ref, pooled_ref, prev_ref, g_ref, n_one_ref, n_two_ref, gr_ref, qkv_ref, mixed_ref, gqkv_ref,
    att_ref, r_one, s_ref, r_two, t_ref, r_three, u_ref, line_ready,
    in_sems, count_sems, cot_sems, pool_sems, one_send, one_recv, two_send, two_recv, three_send, three_recv,
    five_send, five_recv, six_send, six_recv,
):
    rows, width = tok_ref.shape
    crows = cots_ref.shape[0] // 2
    out_slots = crows // 4
    factor = HEAD_DIM ** (-0.5)
    blocks = rows // BLK
    me = lax.axis_index("unit")
    z = lax.axis_index("img")
    units = lax.axis_size("unit")
    nz = lax.axis_size("img")
    chips = units // 2
    nx = min(4, chips)
    ny = chips // nx
    core = lax.rem(me, 2)
    chip = me // 2
    chip_x, chip_y = lax.rem(chip, nx), chip // nx
    half = HALF // 2
    piece = half // chips
    tile = piece // 4
    sibling = me + 1 - 2 * core
    plane = [(dx, dy) for dx in AROUND[nx] for dy in AROUND[ny]][:-1]

    def chip_at(dx, dy):
        return lax.rem(chip_y + dy, ny) * nx + lax.rem(chip_x + dx, nx)

    def fetch(k, source, target):
        copy = pltpu.make_async_copy(source, target, in_sems.at[k])
        copy.start()
        return copy

    def push(source, target, send, recv, **where):
        copy = pltpu.make_async_remote_copy(
            src_ref=source, dst_ref=target, send_sem=send, recv_sem=recv, device_id=where, device_id_type=MESH
        )
        copy.start()
        return copy

    def drain(ref, sem):
        pltpu.make_async_copy(ref, ref, sem).wait()

    get_tok = fetch(0, tok_hbm, tok_ref)
    get_gain_one = fetch(1, gain_one_hbm, gain_one_ref)
    get_w_qkv = fetch(2, w_qkv_hbm, w_qkv_ref)
    get_cot = fetch(3, cot_hbm, cot_ref)
    get_w_out = fetch(4, w_out_hbm, w_out_ref)
    get_gain_two = fetch(5, gain_two_hbm, gain_two_ref)
    get_w_pool = fetch(6, w_pool_hbm, w_pool_ref)

    barrier = pltpu.get_barrier_semaphore()
    reach = nz // 4
    near = [d for d in range(1, nz) if min(d, nz - d) <= reach]
    for d in near:
        pl.semaphore_signal(barrier, inc=1, device_id={"img": lax.rem(z + d, nz)}, device_id_type=MESH)
    for dx, dy in plane:
        for which in range(2):
            there = chip_at(dx, dy) * 2 + which
            pl.semaphore_signal(barrier, inc=1, device_id={"unit": there}, device_id_type=MESH)
    pl.semaphore_signal(barrier, inc=1, device_id={"unit": sibling}, device_id_type=MESH)

    def half_of(part, which):
        return pl.ds(pl.multiple_of(part * HALF + which * half, half), half)

    def pair_send(part):
        push(g_ref.at[half_of(part, 1 - core)], r_one.at[part], one_send.at[part], one_recv.at[part], unit=sibling)

    def pair_add(part):
        drain(r_one.at[part], one_recv.at[part])
        own = g_ref[half_of(part, core), :]
        s_ref[part] = (own.astype(F32) + r_one[part].astype(F32)).astype(BF)
        for k, (dx, dy) in enumerate(plane):
            there = chip_at(dx, dy)
            push(
                s_ref.at[part, pl.ds(pl.multiple_of(there * piece, piece), piece)], r_two.at[part, k],
                two_send.at[part], two_recv.at[part], unit=there * 2 + core,
            )

    def plane_add(part):
        drain(r_two.at[part], two_recv.at[part])
        total = s_ref[part, pl.ds(pl.multiple_of(chip * piece, piece), piece), :].astype(F32)
        for k in range(chips - 1):
            total = total + r_two[part, k].astype(F32)
        t_ref[part] = total.astype(BF)
        for d in range(1, nz):
            there = lax.rem(z + d, nz)
            push(
                t_ref.at[part, pl.ds(pl.multiple_of(lax.rem(there, 4) * tile, tile), tile)], r_three.at[part, z],
                three_send.at[part], three_recv.at[part], img=there,
            )
        r_three[part, z] = t_ref[part, pl.ds(pl.multiple_of(lax.rem(z, 4) * tile, tile), tile), :]

    mine = pl.ds(pl.multiple_of(lax.rem(z, 4) * tile, tile), tile)

    def place(part, which_core, which_chip):
        return pl.ds(pl.multiple_of(part * HALF + which_core * half + which_chip * piece, piece), piece)

    def line_add(part):
        drain(r_three.at[part, pl.ds(0, nz - 1)], three_recv.at[part])
        total = r_three[part, 0].astype(F32)
        for k in range(1, nz):
            total = total + r_three[part, k].astype(F32)
        u_ref[part] = total.astype(BF)
        start = part * HALF + core * half + chip * piece + lax.rem(z, 4) * tile
        here = pl.ds(pl.multiple_of(start, tile), tile)
        for k, (dx, dy) in enumerate(plane + [(0, 0)]):
            for d in (2, 1, nz - 1, 0):
                if k < chips - 1 or d > 0:
                    push(
                        u_ref.at[part], f_ref.at[here], five_send.at[part], five_recv.at[part, k],
                        img=lax.rem(z + d, nz), unit=chip_at(dx, dy) * 2 + core,
                    )
        f_ref[here, :] = u_ref[part]

    def pair_spread(part):
        for k, (dx, dy) in reversed(list(enumerate(plane + [(0, 0)]))):
            there = place(part, core, chip_at(nx - dx, ny - dy))
            if k < chips - 1:
                drain(f_ref.at[there], five_recv.at[part, k])
            else:
                drain(f_ref.at[pl.ds(0, 3 * tile)], five_recv.at[part, k])
            push(f_ref.at[there], f_ref.at[there], six_send.at[part], six_recv.at[part], unit=sibling)

    get_tok.wait()
    get_gain_one.wait()
    n_one, p_one = normalize(tok_ref[...].astype(F32))
    n_one_ref[...] = n_one
    normed = (n_one * gain_one_ref[...]).astype(BF)
    get_w_qkv.wait()
    qkv_ref[...] = nn(normed, w_qkv_ref[...]).astype(BF)

    same = (
        lax.broadcasted_iota(jnp.int32, (HEADS * BLK, BLK), 0) & (BLK - 1)
    ) >> 4 == lax.broadcasted_iota(jnp.int32, (HEADS * BLK, BLK), 1) >> 4
    for b in range(blocks):
        span = slice(b * BLK, (b + 1) * BLK)
        query = head_rows(qkv_ref[span, :width])
        scores = nt(query, qkv_ref[span, width : 2 * width]) * factor
        scores = jnp.where(same, scores, -1e30)
        e = jnp.exp(scores - jnp.max(scores, axis=-1, keepdims=True))
        att = e * (1.0 / jnp.sum(e, axis=-1, keepdims=True))
        att_ref[b] = att
        value = head_rows(qkv_ref[span, 2 * width :])
        mixed_ref[span, :] = nn(heads_to_lanes(att.astype(BF)), value).astype(BF)

    get_cot.wait()
    cots_ref[:crows, :] = cot_ref[...].reshape(crows, cots_ref.shape[1])
    counts_ref[me] = jnp.full((8, LANES), live_ref[0, 0], jnp.int32)
    pl.semaphore_wait(barrier, len(near) + units - 1)
    for d in (reach, nz - reach):
        pl.semaphore_signal(line_ready, inc=1, device_id={"img": lax.rem(z + d, nz)}, device_id_type=MESH)
    for dx, dy in plane:
        for which in range(2):
            there = chip_at(dx, dy) * 2 + which
            push(counts_ref.at[me], counts_ref.at[me], count_sems.at[0], count_sems.at[1], unit=there)
    push(counts_ref.at[me], counts_ref.at[me], count_sems.at[0], count_sems.at[1], unit=sibling)
    cot_copy = push(
        cots_ref.at[pl.ds(0, crows)], cots_ref.at[pl.ds(crows, crows)], cot_sems.at[0], cot_sems.at[1],
        unit=lax.rem(me + units - 1, units),
    )

    get_w_out.wait()
    get_gain_two.wait()
    n_two, p_two = normalize(tok_ref[...].astype(F32) + nn(mixed_ref[...], w_out_ref[...]))
    n_two_ref[...] = n_two
    y = n_two * gain_two_ref[...]
    high = y.astype(BF)
    low = (y - high.astype(F32)).astype(BF)

    get_w_pool.wait()
    others = counts_ref.at[pl.ds(0, units - 1)]
    drain(others, count_sems.at[1])
    before = jnp.zeros((8, LANES), jnp.int32)
    for k in range(units):
        before = before + jnp.where(k < me, counts_ref[k], 0)
    shift = before[0:1, :] - me * out_slots
    live = live_ref[0, 0]
    ranked = 2 * crows
    gather = selection((ranked, rows), 1, shift[:, 0:1], live)
    spread = selection((rows, ranked), 0, shift[:, :ranked], live)
    grouped = (nn(gather, high) + nn(gather, low)).astype(BF)
    cot_copy.wait_recv()
    cots = cots_ref[...]
    grad_pool = tn(grouped, cots).astype(BF)
    g_scaled = nt(nn(spread, cots).astype(BF), w_pool_ref[...])
    n_two = n_two_ref[...]
    g_ref[2016:2048, :] = gain_rows(jnp.sum(g_scaled * n_two, axis=0, keepdims=True))
    g_resid = norm_back(g_scaled * gain_two_ref[...], n_two, p_two)
    gr_ref[...] = g_resid
    resid_b = g_resid.astype(BF)
    grad_out = tn(mixed_ref[...], resid_b).astype(BF)
    for k in range(4):
        g_ref[width * k : width * (k + 1), :] = grad_pool[:, LANES * k : LANES * (k + 1)]
    g_ref[width * 4 : width * 5, :] = jnp.concatenate(
        [grad_pool[:, 512:576], grad_out[:, 256:288], jnp.zeros((width, 32), BF)], axis=1
    )
    g_ref[width * 5 : width * 6, :] = grad_out[:, :128]
    g_ref[width * 6 : width * 7, :] = grad_out[:, 128:256]
    pair_send(0)

    mixed_ref[...] = nt(resid_b, w_out_ref[...]).astype(BF)
    for b in range(blocks):
        span = slice(b * BLK, (b + 1) * BLK)
        att = att_ref[b]
        g_mixed = head_rows(mixed_ref[span, :])
        g_att = nt(g_mixed, qkv_ref[span, 2 * width :])
        g_value = tn(att.astype(BF), g_mixed).astype(BF)
        g_scores = (att * (g_att - jnp.sum(g_att * att, axis=-1, keepdims=True)) * factor).astype(BF)
        g_query = nn(heads_to_lanes(g_scores), head_rows(qkv_ref[span, width : 2 * width])).astype(BF)
        g_key = tn(g_scores, head_rows(qkv_ref[span, :width])).astype(BF)
        gqkv_ref[span, :] = jnp.concatenate([g_query, g_key, g_value], axis=1)
        if b == blocks - 2:
            pair_add(0)

    g_qkv = gqkv_ref[...]
    n_one = n_one_ref[...]
    normed = (n_one * gain_one_ref[...]).astype(BF)
    grad_qkv = tn(normed, g_qkv).astype(BF)
    for k in range(6):
        g_ref[HALF + width * k : HALF + width * (k + 1), :] = grad_qkv[:, LANES * k : LANES * (k + 1)]
    g_ref[HALF + width * 6 : HALF + width * 7, :] = jnp.concatenate(
        [grad_qkv[:, 768:864], jnp.zeros((width, 32), BF)], axis=1
    )
    g_normed = nt(g_qkv, w_qkv_ref[...])
    g_ref[HALF + 2016 : HALF + 2048, :] = gain_rows(jnp.sum(g_normed * n_one, axis=0, keepdims=True))
    pair_send(1)
    pooled_ref[...] = nn(grouped, w_pool_ref[...]).astype(BF)
    pooled_copy = push(
        pooled_ref.at[pl.ds(crows, crows)], prev_ref, pool_sems.at[0], pool_sems.at[1],
        unit=lax.rem(me + 1, units),
    )
    g_input = norm_back(g_normed * gain_one_ref[...], n_one, p_one)
    grad_tokens_ref[...] = (gr_ref[...] + g_input).astype(BF)

    pair_add(1)
    pl.semaphore_wait(line_ready, 2)
    plane_add(0)
    pooled_copy.wait_recv()
    pooled_out[...] = pooled_ref[:crows, :] + prev_ref[...]
    plane_add(1)
    line_add(0)
    line_add(1)
    pair_spread(0)
    pair_spread(1)

    for part in range(2):
        drain(g_ref.at[pl.ds(0, half)], one_send.at[part])
        drain(r_two.at[part], two_send.at[part])
        drain(r_three.at[part, pl.ds(0, nz - 1)], three_send.at[part])
        drain(f_ref.at[pl.ds(0, half - tile)], five_send.at[part])
        drain(f_ref.at[pl.ds(0, half)], six_send.at[part])
        drain(f_ref.at[pl.ds(0, half)], six_recv.at[part])
    drain(others, count_sems.at[0])
    cot_copy.wait_send()
    pooled_copy.wait_send()


def unpack_kernel(
    scale, f_ref, pooled_ref, tok_ref, out_ref, grad_tokens_ref, qkv_ref, go_ref, pool_ref, one_ref, two_ref
):
    width = go_ref.shape[0]

    def rows(start, count):
        return f_ref[start : start + count, :].astype(F32) * scale

    for k in range(7):
        early = rows(width * k, width)
        late = rows(HALF + width * k, width)
        if k < 6:
            qkv_ref[:, LANES * k : LANES * (k + 1)] = late
        else:
            qkv_ref[:, 768:864] = late[:, :96]
        if k < 4:
            pool_ref[:, LANES * k : LANES * (k + 1)] = early
        elif k == 4:
            pool_ref[:, 512:576] = early[:, :64]
            go_ref[:, 256:288] = early[:, 64:96]
        else:
            go_ref[:, LANES * (k - 5) : LANES * (k - 4)] = early
    for start, ref in ((2016, two_ref), (HALF + 2016, one_ref)):
        last = rows(start, 32)
        ref[...] = jnp.concatenate([last[0:1], last[1:2], last[2:3, :32]], axis=1).reshape(ref.shape)
    out_ref[...] = pooled_ref[...].reshape(out_ref.shape)
    grad_tokens_ref[...] = tok_ref[...]


def whole(count, space=pltpu.VMEM):
    return [pl.BlockSpec(memory_space=space)] * count


def local(tokens, live, cotangent, w_qkv, w_out, w_pool, gain_one, gain_two):
    img_dev, slots, token_count, width = tokens.shape
    out_slots, out_width = cotangent.shape[1], cotangent.shape[3]
    units, nz = lax.axis_size("unit"), lax.axis_size("img")
    chips = units // 2
    rows = slots * token_count
    crows = out_slots * 4
    piece = HALF // 2 // chips
    dma, vmem = pltpu.SemaphoreType.DMA, pltpu.VMEM

    def sd(shape, dtype):
        return jax.ShapeDtypeStruct(shape, dtype)

    f, pooled, grad_tok = pl.pallas_call(
        main_kernel,
        out_shape=(vmem((2 * HALF, LANES), BF), vmem((crows, out_width), BF), vmem((rows, width), BF)),
        in_specs=[pl.BlockSpec(memory_space=pltpu.SMEM)] + whole(7, pltpu.HBM),
        out_specs=whole(3),
        scratch_shapes=[
            vmem((rows, width), BF),
            vmem((out_slots, 4, out_width), BF),
            vmem(w_qkv.shape, BF),
            vmem(w_out.shape, BF),
            vmem(w_pool.shape, BF),
            vmem(gain_one.shape, F32),
            vmem(gain_two.shape, F32),
            vmem((units, 8, LANES), jnp.int32),
            vmem((2 * crows, out_width), BF),
            vmem((2 * crows, out_width), BF),
            vmem((crows, out_width), BF),
            vmem((2 * HALF, LANES), BF),
            vmem((rows, width), F32),
            vmem((rows, width), F32),
            vmem((rows, width), F32),
            vmem((rows, 3 * width), BF),
            vmem((rows, width), BF),
            vmem((rows, 3 * width), BF),
            vmem((rows // BLK, HEADS * BLK, BLK), F32),
            vmem((2, HALF // 2, LANES), BF),
            vmem((2, HALF // 2, LANES), BF),
            vmem((2, chips - 1, piece, LANES), BF),
            vmem((2, piece, LANES), BF),
            vmem((2, nz, piece // 4, LANES), BF),
            vmem((2, piece // 4, LANES), BF),
            pltpu.SemaphoreType.REGULAR,
            dma((7,)), dma((2,)), dma((2,)), dma((2,)), dma((2,)), dma((2,)), dma((2,)), dma((2,)), dma((2,)),
            dma((2,)), dma((2,)), dma((2, chips)), dma((2,)), dma((2,)),
        ],
        compiler_params=pltpu.CompilerParams(collective_id=0, has_side_effects=True, vmem_limit_bytes=VMEM_LIMIT),
        name="main",
    )(
        live, tokens.reshape(rows, width), cotangent.reshape(out_slots, 4, out_width), w_qkv, w_out, w_pool,
        gain_one, gain_two,
    )

    scale = 1.0 / math.sqrt(img_dev * nz * out_slots * units)
    out, grad_tokens, grad_qkv, grad_out, grad_pool, one, two = pl.pallas_call(
        functools.partial(unpack_kernel, scale),
        out_shape=(
            sd((out_slots, 4, out_width), BF), sd((rows, width), BF), sd((width, 3 * width), F32),
            sd((width, width), F32), sd((width, out_width), F32), sd((width,), F32), sd((width,), F32),
        ),
        in_specs=whole(3),
        out_specs=whole(7),
        compiler_params=pltpu.CompilerParams(vmem_limit_bytes=UNPACK_LIMIT),
        name="unpack",
    )(f, pooled, grad_tok)
    return (
        out.reshape(cotangent.shape), grad_tokens.reshape(tokens.shape), grad_qkv, grad_out, grad_pool, one, two,
    )


def solution(mesh):
    return jax.shard_map(
        local,
        mesh=mesh,
        in_specs=(
            P("img", "unit", None, None), P("img", "unit"), P("img", "unit", None, None),
            P(), P(), P(), P(), P(),
        ),
        out_specs=(P("img", "unit", None, None), P("img", "unit", None, None), P(), P(), P(), P(), P()),
        check_vma=False,
    )
```

```python
import functools
import math

import jax
import jax.numpy as jnp
from jax import lax
from jax.experimental import pallas as pl
from jax.experimental.pallas import tpu as pltpu
from jax.sharding import PartitionSpec as P

HEADS = 4
HEAD_DIM = 72
EPSILON = 1e-06
BF = jnp.bfloat16
F32 = jnp.float32
MESH = pl.DeviceIdType.MESH
TOK = 16
BLK = 128
LANES = 128
HALF = 2048
AROUND = {1: (0,), 2: (1, 0), 4: (2, 1, 3, 0)}
VMEM_LIMIT = 62 * 1024 * 1024
UNPACK_LIMIT = 24 * 1024 * 1024


def nn(a, b):
    return lax.dot_general(a, b, (((1,), (0,)), ((), ())), preferred_element_type=F32)


def nt(a, b):
    return lax.dot_general(a, b, (((1,), (1,)), ((), ())), preferred_element_type=F32)


def tn(a, b):
    return lax.dot_general(a, b, (((0,), (0,)), ((), ())), preferred_element_type=F32)


def normalize(values):
    centred = values - jnp.mean(values, axis=-1, keepdims=True)
    inv_scale = lax.rsqrt(jnp.mean(centred * centred, axis=-1, keepdims=True) + EPSILON)
    return centred * inv_scale, inv_scale


def norm_back(grad_norm, normed_v, inv_scale):
    first = jnp.mean(grad_norm, axis=-1, keepdims=True)
    second = jnp.mean(grad_norm * normed_v, axis=-1, keepdims=True)
    return inv_scale * (grad_norm - first - normed_v * second)


def slot_map(shape, token_dim, live):
    token = lax.broadcasted_iota(jnp.int32, shape, token_dim)
    row = lax.broadcasted_iota(jnp.int32, shape, 1 - token_dim) & (LANES - 1)
    slot = token >> 4
    group = ((token >> 3) & 1) * 2 + ((token >> 1) & 1)
    return jnp.where(slot < live, row - slot * 4 - group, -1)


def select(mapped, shift):
    return jnp.where(mapped == shift, 0.25, 0.0).astype(BF)


def head_rows(block):
    lane = lax.broadcasted_iota(jnp.int32, (1, block.shape[1]), 1)
    parts = []
    for head in range(HEADS):
        mine = (lane >= head * HEAD_DIM) & (lane < (head + 1) * HEAD_DIM)
        parts.append(block * jnp.where(mine, 1.0, 0.0).astype(BF))
    return jnp.concatenate(parts, axis=0)


def heads_to_lanes(rows):
    return jnp.concatenate([rows[h * BLK : (h + 1) * BLK] for h in range(HEADS)], axis=1)


def split(values):
    high = values.astype(BF)
    return high, (values - high.astype(F32)).astype(BF)


def scores_back(att, g_att, keys):
    inner = jnp.sum(g_att * att, axis=keys, keepdims=True)
    return (att * (g_att - inner) * HEAD_DIM ** (-0.5)).astype(BF)


def gain_rows(total):
    row = lax.broadcasted_iota(jnp.int32, (32, LANES), 0)
    last = jnp.concatenate([total[:, 256:], jnp.zeros((1, 96), F32)], axis=1)
    out = jnp.where(row == 0, total[:, :128], 0.0)
    out = jnp.where(row == 1, total[:, 128:256], out)
    return jnp.where(row == 2, last, out).astype(BF)


def main_kernel(
    live_ref, tok_hbm, cot_hbm, w_qkv_hbm, w_out_hbm, w_pool_hbm, gain_one_hbm, gain_two_hbm,
    f_ref, pooled_out, grad_tokens_ref,
    tok_ref, cot_ref, w_qkv_ref, w_out_ref, w_pool_ref, gain_one_ref, gain_two_ref,
    counts_ref, cots_ref, pooled_ref, prev_ref, g_ref, n_one_ref, n_two_ref, gr_ref, qkv_ref, mixed_ref, gqkv_ref, gmix_ref, to_rows, to_tokens, h_rows,
    att_ref, att_t, q_rows, k_rows, normed_t, mixed_t, r_one, s_ref, r_two, t_ref, r_three, u_ref, line_ready,
    in_sems, count_sems, cot_sems, pool_sems, one_send, one_recv, two_send, two_recv, three_send, three_recv,
    five_send, five_recv, six_send, six_recv, line_send,
):
    rows, width = tok_ref.shape
    crows = cots_ref.shape[0] // 2
    out_slots = crows // 4
    factor = HEAD_DIM ** (-0.5)
    blocks = rows // BLK
    me = lax.axis_index("unit")
    z = lax.axis_index("img")
    units = lax.axis_size("unit")
    nz = lax.axis_size("img")
    chips = units // 2
    nx = min(4, chips)
    ny = chips // nx
    core = lax.rem(me, 2)
    chip = me // 2
    chip_x, chip_y = lax.rem(chip, nx), chip // nx
    half = HALF // 2
    piece = half // chips
    tile = piece // 4
    sibling = me + 1 - 2 * core
    plane = [(dx, dy) for dx in AROUND[nx] for dy in AROUND[ny]][:-1]

    def chip_at(dx, dy):
        return lax.rem(chip_y + dy, ny) * nx + lax.rem(chip_x + dx, nx)

    def fetch(k, source, target):
        copy = pltpu.make_async_copy(source, target, in_sems.at[k])
        copy.start()
        return copy

    def push(source, target, send, recv, **where):
        copy = pltpu.make_async_remote_copy(
            src_ref=source, dst_ref=target, send_sem=send, recv_sem=recv, device_id=where, device_id_type=MESH
        )
        copy.start()
        return copy

    def drain(ref, sem):
        pltpu.make_async_copy(ref, ref, sem).wait()

    barrier = pltpu.get_barrier_semaphore()
    reach = nz // 4
    near = [d for d in range(1, nz) if min(d, nz - d) <= reach]
    for d in near:
        pl.semaphore_signal(barrier, inc=1, device_id={"img": lax.rem(z + d, nz)}, device_id_type=MESH)
    for dx, dy in plane:
        for which in range(2):
            there = chip_at(dx, dy) * 2 + which
            pl.semaphore_signal(barrier, inc=1, device_id={"unit": there}, device_id_type=MESH)
    pl.semaphore_signal(barrier, inc=1, device_id={"unit": sibling}, device_id_type=MESH)

    get_tok = fetch(0, tok_hbm, tok_ref)
    get_gain_one = fetch(1, gain_one_hbm, gain_one_ref)
    get_w_qkv = fetch(2, w_qkv_hbm, w_qkv_ref)
    get_cot = fetch(3, cot_hbm, cot_ref)
    get_w_out = fetch(4, w_out_hbm, w_out_ref)
    get_gain_two = fetch(5, gain_two_hbm, gain_two_ref)
    get_w_pool = fetch(6, w_pool_hbm, w_pool_ref)

    def half_of(part, which):
        return pl.ds(pl.multiple_of(part * HALF + which * half, half), half)

    def pair_send(part):
        count = half - 32 * part
        push(
            g_ref.at[pl.ds(pl.multiple_of(part * HALF + (1 - core) * half, half), count)],
            r_one.at[part, pl.ds(0, count)], one_send.at[part], one_recv.at[part], unit=sibling,
        )

    def pair_send_last():
        start = HALF + (1 - core) * half + half - 32
        push(
            g_ref.at[pl.ds(pl.multiple_of(start, 32), 32)], r_one.at[1, pl.ds(half - 32, 32)],
            one_send.at[2], one_recv.at[2], unit=sibling,
        )

    def pair_add(part):
        drain(r_one.at[part, pl.ds(0, half - 32 * part)], one_recv.at[part])
        if part == 1:
            drain(r_one.at[1, pl.ds(half - 32, 32)], one_recv.at[2])
        own = g_ref[half_of(part, core), :]
        s_ref[part] = (own.astype(F32) + r_one[part].astype(F32)).astype(BF)
        for k, (dx, dy) in enumerate(plane):
            there = chip_at(dx, dy)
            push(
                s_ref.at[part, pl.ds(pl.multiple_of(there * piece, piece), piece)], r_two.at[part, k],
                two_send.at[part], two_recv.at[part], unit=there * 2 + core,
            )

    def plane_add(part):
        drain(r_two.at[part], two_recv.at[part])
        total = s_ref[part, pl.ds(pl.multiple_of(chip * piece, piece), piece), :].astype(F32)
        for k in range(chips - 1):
            total = total + r_two[part, k].astype(F32)
        t_ref[part] = total.astype(BF)
        for d in sorted(range(1, nz), key=lambda d: -min(d, nz - d)):
            there = lax.rem(z + d, nz)
            push(
                t_ref.at[part, pl.ds(pl.multiple_of(lax.rem(there, 4) * tile, tile), tile)], r_three.at[part, z],
                three_send.at[part], three_recv.at[part], img=there,
            )
        r_three[part, z] = t_ref[part, pl.ds(pl.multiple_of(lax.rem(z, 4) * tile, tile), tile), :]

    mine = pl.ds(pl.multiple_of(lax.rem(z, 4) * tile, tile), tile)

    def place(part, which_core, which_chip):
        return pl.ds(pl.multiple_of(part * HALF + which_core * half + which_chip * piece, piece), piece)

    def line_add(part):
        drain(r_three.at[part, pl.ds(0, nz - 1)], three_recv.at[part])
        total = r_three[part, 0].astype(F32)
        for k in range(1, nz):
            total = total + r_three[part, k].astype(F32)
        u_ref[part] = total.astype(BF)
        start = part * HALF + core * half + chip * piece + lax.rem(z, 4) * tile
        here = pl.ds(pl.multiple_of(start, tile), tile)
        if part == 0:
            for d in (2, 1, nz - 1):
                push(
                    u_ref.at[part], f_ref.at[here], line_send, five_recv.at[part, chips - 1],
                    img=lax.rem(z + d, nz),
                )
            f_ref[here, :] = u_ref[part]
            return
        for k, (dx, dy) in enumerate(plane + [(0, 0)]):
            for d in (2, 1, nz - 1, 0):
                if k < chips - 1 or d > 0:
                    push(
                        u_ref.at[part], f_ref.at[here], five_send.at[part], five_recv.at[part, k],
                        img=lax.rem(z + d, nz), unit=chip_at(dx, dy) * 2 + core,
                    )
        f_ref[here, :] = u_ref[part]

    def plane_spread(part):
        drain(f_ref.at[pl.ds(0, 3 * tile)], five_recv.at[part, chips - 1])
        own = f_ref.at[place(part, core, chip)]
        for k, (dx, dy) in enumerate(plane):
            push(own, own, five_send.at[part], five_recv.at[part, k], unit=chip_at(dx, dy) * 2 + core)

    def pair_spread(part):
        for k, (dx, dy) in reversed(list(enumerate(plane + [(0, 0)]))):
            there = place(part, core, chip_at(nx - dx, ny - dy))
            if k < chips - 1:
                drain(f_ref.at[there], five_recv.at[part, k])
            elif part == 1:
                drain(f_ref.at[pl.ds(0, 3 * tile)], five_recv.at[part, k])
            push(f_ref.at[there], f_ref.at[there], six_send.at[part], six_recv.at[part], unit=sibling)

    get_tok.wait()
    get_gain_one.wait()
    n_one, p_one = normalize(tok_ref[...].astype(F32))
    n_one_ref[...] = n_one
    normed = (n_one * gain_one_ref[...]).astype(BF)
    get_w_qkv.wait()
    qkv_ref[...] = nn(normed, w_qkv_ref[...]).astype(BF)

    get_cot.wait()
    cots_ref[:crows, :] = cot_ref[...].reshape(crows, cots_ref.shape[1])
    counts_ref[me] = jnp.full((1, LANES), live_ref[0, 0], jnp.int32)
    pl.semaphore_wait(barrier, len(near) + units - 1)
    for d in (reach, nz - reach):
        pl.semaphore_signal(line_ready, inc=1, device_id={"img": lax.rem(z + d, nz)}, device_id_type=MESH)
    for dx, dy in plane:
        for which in range(2):
            there = chip_at(dx, dy) * 2 + which
            push(counts_ref.at[me], counts_ref.at[me], count_sems.at[0], count_sems.at[1], unit=there)
    push(counts_ref.at[me], counts_ref.at[me], count_sems.at[0], count_sems.at[1], unit=sibling)
    cot_copy = push(
        cots_ref.at[pl.ds(0, crows)], cots_ref.at[pl.ds(crows, crows)], cot_sems.at[0], cot_sems.at[1],
        unit=lax.rem(me + units - 1, units),
    )

    same = (
        lax.broadcasted_iota(jnp.int32, (HEADS * BLK, BLK), 0) & (BLK - 1)
    ) >> 4 == lax.broadcasted_iota(jnp.int32, (HEADS * BLK, BLK), 1) >> 4
    for b in range(blocks):
        span = slice(b * BLK, (b + 1) * BLK)
        q_rows[b] = head_rows(qkv_ref[span, :width])
        k_rows[b] = head_rows(qkv_ref[span, width : 2 * width])
        scores = nt(q_rows[b], qkv_ref[span, width : 2 * width]) * factor
        scores = jnp.where(same, scores, -1e30)
        e = jnp.exp(scores - jnp.max(scores, axis=-1, keepdims=True))
        att = e * (1.0 / jnp.sum(e, axis=-1, keepdims=True))
        att_ref[b] = att
        att_t[b] = att.astype(BF).T
        value = head_rows(qkv_ref[span, 2 * width :])
        mixed_ref[span, :] = nn(heads_to_lanes(att.astype(BF)), value).astype(BF)
    normed_t[...] = normed.T

    get_w_out.wait()
    get_gain_two.wait()
    n_two, p_two = normalize(tok_ref[...].astype(F32) + nn(mixed_ref[...], w_out_ref[...]))
    n_two_ref[...] = n_two
    high, low = split(n_two)
    mixed_t[...] = mixed_ref[...].T
    live = live_ref[0, 0]
    to_rows[...] = slot_map(to_rows.shape, 1, live)
    to_tokens[...] = slot_map(to_tokens.shape, 0, live)
    get_w_pool.wait()
    cot_copy.wait_recv()
    cots = cots_ref[...]
    g_grouped = nt(cots, w_pool_ref[...])
    h_grouped = g_grouped * gain_two_ref[...]
    h_high, h_low = split(h_grouped - jnp.mean(h_grouped, axis=-1, keepdims=True))
    gap = jnp.zeros((LANES - h_high.shape[0], width), BF)
    h_rows[...] = jnp.concatenate([h_high, gap, h_low, gap], axis=0)

    others = counts_ref.at[pl.ds(0, units - 1)]
    drain(others, count_sems.at[1])
    before = jnp.zeros((1, LANES), jnp.int32)
    for k in range(units):
        before = before + jnp.where(k < me, counts_ref[k], 0)
    shift = (before[:, 0:1] - me * out_slots) * 4

    h = nn(select(to_tokens[...], shift), h_rows[...])
    n_two = n_two_ref[...]
    g_resid = p_two * (h - n_two * jnp.mean(h * n_two, axis=-1, keepdims=True))
    gr_ref[...] = g_resid
    resid_b = g_resid.astype(BF)

    gather = select(to_rows[...], shift)
    mean_two = nn(gather, high) + nn(gather, low)
    grouped = (mean_two * gain_two_ref[...]).astype(BF)
    g_ref[2016:2048, :] = gain_rows(jnp.sum(g_grouped * mean_two, axis=0, keepdims=True))
    grad_pool = tn(grouped, cots).astype(BF)
    grad_out = nn(mixed_t[...], resid_b).astype(BF)
    for k in range(4):
        g_ref[width * k : width * (k + 1), :] = grad_pool[:, LANES * k : LANES * (k + 1)]
    g_ref[width * 4 : width * 5, :] = jnp.concatenate(
        [grad_pool[:, 512:576], grad_out[:, 256:288], jnp.zeros((width, 32), BF)], axis=1
    )
    g_ref[width * 5 : width * 6, :] = grad_out[:, :128]
    g_ref[width * 6 : width * 7, :] = grad_out[:, 128:256]
    pair_send(0)

    gmix_ref[...] = nt(resid_b, w_out_ref[...]).astype(BF)

    def scores_of(b):
        span = slice(b * BLK, (b + 1) * BLK)
        rows_b = head_rows(gmix_ref[span, :])
        return rows_b, nt(rows_b, qkv_ref[span, 2 * width :])

    ahead = scores_of(0)
    for b in range(blocks):
        span = slice(b * BLK, (b + 1) * BLK)
        g_mixed, g_att = ahead
        if b + 1 < blocks:
            ahead = scores_of(b + 1)
        g_value = nn(att_t[b], g_mixed).astype(BF)
        g_scores = scores_back(att_ref[b], g_att, -1)
        g_query = nn(heads_to_lanes(g_scores), k_rows[b]).astype(BF)
        g_key = tn(g_scores, q_rows[b]).astype(BF)
        gqkv_ref[span, :] = jnp.concatenate([g_query, g_key, g_value], axis=1)
        if b == blocks - 2:
            pair_add(0)

    g_qkv = gqkv_ref[...]
    n_one = n_one_ref[...]
    grad_qkv = nn(normed_t[...], g_qkv).astype(BF)
    for k in range(6):
        g_ref[HALF + width * k : HALF + width * (k + 1), :] = grad_qkv[:, LANES * k : LANES * (k + 1)]
    g_ref[HALF + width * 6 : HALF + width * 7, :] = jnp.concatenate(
        [grad_qkv[:, 768:864], jnp.zeros((width, 32), BF)], axis=1
    )
    pair_send(1)
    g_normed = nt(g_qkv, w_qkv_ref[...])
    g_ref[HALF + 2016 : HALF + 2048, :] = gain_rows(jnp.sum(g_normed * n_one, axis=0, keepdims=True))
    pair_send_last()
    pooled_ref[...] = nn(grouped, w_pool_ref[...]).astype(BF)
    pooled_copy = push(
        pooled_ref.at[pl.ds(crows, crows)], prev_ref, pool_sems.at[0], pool_sems.at[1],
        unit=lax.rem(me + 1, units),
    )
    g_input = norm_back(g_normed * gain_one_ref[...], n_one, p_one)
    grad_tokens_ref[...] = (gr_ref[...] + g_input).astype(BF)

    pair_add(1)
    pl.semaphore_wait(line_ready, 2)
    plane_add(0)
    pooled_copy.wait_recv()
    pooled_out[...] = pooled_ref[:crows, :] + prev_ref[...]
    plane_add(1)
    line_add(0)
    plane_spread(0)
    line_add(1)
    pair_spread(0)
    pair_spread(1)

    for part in range(2):
        drain(g_ref.at[pl.ds(0, half - 32 * part)], one_send.at[part])
        drain(r_two.at[part], two_send.at[part])
        drain(r_three.at[part, pl.ds(0, nz - 1)], three_send.at[part])
        drain(f_ref.at[pl.ds(0, half - (piece, tile)[part])], five_send.at[part])
        drain(f_ref.at[pl.ds(0, half)], six_send.at[part])
        drain(f_ref.at[pl.ds(0, half)], six_recv.at[part])
    drain(g_ref.at[pl.ds(0, 32)], one_send.at[2])
    drain(f_ref.at[pl.ds(0, 3 * tile)], line_send)
    drain(others, count_sems.at[0])
    cot_copy.wait_send()
    pooled_copy.wait_send()


def unpack_kernel(
    scale, f_ref, pooled_ref, tok_ref, out_hbm, grad_tokens_hbm, qkv_hbm, go_hbm, pool_hbm, one_hbm, two_hbm,
    out_ref, qkv_ref, go_ref, pool_ref, one_ref, two_ref, sems,
):
    width = go_ref.shape[0]
    copies = []

    def store(source, target):
        copy = pltpu.make_async_copy(source, target, sems.at[len(copies)])
        copy.start()
        copies.append(copy)

    store(tok_ref, grad_tokens_hbm)
    step = width // 3
    for r in range(0, width, step):
        span = slice(r, r + step)

        def rows(start):
            return f_ref[start + r : start + r + step, :].astype(F32) * scale

        for k in range(6):
            qkv_ref[span, LANES * k : LANES * (k + 1)] = rows(HALF + width * k)
        qkv_ref[span, 768:864] = rows(HALF + width * 6)[:, :96]
        store(qkv_ref.at[pl.ds(r, step)], qkv_hbm.at[pl.ds(r, step)])
        for k in range(4):
            pool_ref[span, LANES * k : LANES * (k + 1)] = rows(width * k)
        both = rows(width * 4)
        pool_ref[span, 512:576] = both[:, :64]
        store(pool_ref.at[pl.ds(r, step)], pool_hbm.at[pl.ds(r, step)])
        go_ref[span, 256:288] = both[:, 64:96]
        for k in range(2):
            go_ref[span, LANES * k : LANES * (k + 1)] = rows(width * (k + 5))
        store(go_ref.at[pl.ds(r, step)], go_hbm.at[pl.ds(r, step)])
    for start, ref, target in ((2016, two_ref, two_hbm), (HALF + 2016, one_ref, one_hbm)):
        last = f_ref[start : start + 32, :].astype(F32) * scale
        ref[...] = jnp.concatenate([last[0:1], last[1:2], last[2:3, :32]], axis=1).reshape(ref.shape)
        store(ref, target)
    out_ref[...] = pooled_ref[...].reshape(out_ref.shape)
    store(out_ref, out_hbm)
    for copy in copies:
        copy.wait()


def whole(count, space=pltpu.VMEM):
    return [pl.BlockSpec(memory_space=space)] * count


def local(tokens, live, cotangent, w_qkv, w_out, w_pool, gain_one, gain_two):
    img_dev, slots, token_count, width = tokens.shape
    out_slots, out_width = cotangent.shape[1], cotangent.shape[3]
    units, nz = lax.axis_size("unit"), lax.axis_size("img")
    chips = units // 2
    rows = slots * token_count
    crows = out_slots * 4
    piece = HALF // 2 // chips
    dma, vmem = pltpu.SemaphoreType.DMA, pltpu.VMEM

    def sd(shape, dtype):
        return jax.ShapeDtypeStruct(shape, dtype)

    f, pooled, grad_tok = pl.pallas_call(
        main_kernel,
        out_shape=(vmem((2 * HALF, LANES), BF), vmem((crows, out_width), BF), vmem((rows, width), BF)),
        in_specs=[pl.BlockSpec(memory_space=pltpu.SMEM)] + whole(7, pltpu.HBM),
        out_specs=whole(3),
        scratch_shapes=[
            vmem((rows, width), BF),
            vmem((out_slots, 4, out_width), BF),
            vmem(w_qkv.shape, BF),
            vmem(w_out.shape, BF),
            vmem(w_pool.shape, BF),
            vmem(gain_one.shape, F32),
            vmem(gain_two.shape, F32),
            vmem((units, 1, LANES), jnp.int32),
            vmem((2 * crows, out_width), BF),
            vmem((2 * crows, out_width), BF),
            vmem((crows, out_width), BF),
            vmem((2 * HALF, LANES), BF),
            vmem((rows, width), F32),
            vmem((rows, width), F32),
            vmem((rows, width), F32),
            vmem((rows, 3 * width), BF),
            vmem((rows, width), BF),
            vmem((rows, 3 * width), BF),
            vmem((rows, width), BF),
            vmem((2 * crows, rows), jnp.int32),
            vmem((rows, 2 * LANES), jnp.int32),
            vmem((2 * LANES, width), BF),
            vmem((rows // BLK, HEADS * BLK, BLK), F32),
            vmem((rows // BLK, BLK, HEADS * BLK), BF),
            vmem((rows // BLK, HEADS * BLK, width), BF),
            vmem((rows // BLK, HEADS * BLK, width), BF),
            vmem((width, rows), BF),
            vmem((width, rows), BF),
            vmem((2, HALF // 2, LANES), BF),
            vmem((2, HALF // 2, LANES), BF),
            vmem((2, chips - 1, piece, LANES), BF),
            vmem((2, piece, LANES), BF),
            vmem((2, nz, piece // 4, LANES), BF),
            vmem((2, piece // 4, LANES), BF),
            pltpu.SemaphoreType.REGULAR,
            dma((7,)), dma((2,)), dma((2,)), dma((2,)), dma((3,)), dma((3,)), dma((2,)), dma((2,)), dma((2,)),
            dma((2,)), dma((2,)), dma((2, chips)), dma((2,)), dma((2,)), dma,
        ],
        compiler_params=pltpu.CompilerParams(collective_id=0, has_side_effects=True, vmem_limit_bytes=VMEM_LIMIT),
        name="main",
    )(
        live, tokens.reshape(rows, width), cotangent.reshape(out_slots, 4, out_width), w_qkv, w_out, w_pool,
        gain_one, gain_two,
    )

    scale = 1.0 / math.sqrt(img_dev * nz * out_slots * units)
    out, grad_tokens, grad_qkv, grad_out, grad_pool, one, two = pl.pallas_call(
        functools.partial(unpack_kernel, scale),
        out_shape=(
            sd((out_slots, 4, out_width), BF), sd((rows, width), BF), sd((width, 3 * width), F32),
            sd((width, width), F32), sd((width, out_width), F32), sd((width,), F32), sd((width,), F32),
        ),
        in_specs=whole(3),
        out_specs=whole(7, pl.ANY),
        scratch_shapes=[
            vmem((out_slots, 4, out_width), BF), vmem((width, 3 * width), F32), vmem((width, width), F32),
            vmem((width, out_width), F32), vmem((width,), F32), vmem((width,), F32), dma((13,)),
        ],
        compiler_params=pltpu.CompilerParams(vmem_limit_bytes=UNPACK_LIMIT),
        name="unpack",
    )(f, pooled, grad_tok)
    return (
        out.reshape(cotangent.shape), grad_tokens.reshape(tokens.shape), grad_qkv, grad_out, grad_pool, one, two,
    )


def solution(mesh):
    return jax.shard_map(
        local,
        mesh=mesh,
        in_specs=(
            P("img", "unit", None, None), P("img", "unit"), P("img", "unit", None, None),
            P(), P(), P(), P(), P(),
        ),
        out_specs=(P("img", "unit", None, None), P("img", "unit", None, None), P(), P(), P(), P(), P()),
        check_vma=False,
    )
```

```python
import functools
import math

import jax
import jax.numpy as jnp
from jax import lax
from jax.experimental import pallas as pl
from jax.experimental.pallas import tpu as pltpu
from jax.sharding import PartitionSpec as P

HEADS = 4
HEAD_DIM = 72
EPSILON = 1e-06
BF = jnp.bfloat16
F32 = jnp.float32
MESH = pl.DeviceIdType.MESH
TOK = 16
BLK = 128
LANES = 128
HALF = 2048
AROUND = {1: (0,), 2: (1, 0), 4: (2, 1, 3, 0)}
VMEM_LIMIT = 62 * 1024 * 1024
UNPACK_LIMIT = 24 * 1024 * 1024


def nn(a, b):
    return lax.dot_general(a, b, (((1,), (0,)), ((), ())), preferred_element_type=F32)


def nt(a, b):
    return lax.dot_general(a, b, (((1,), (1,)), ((), ())), preferred_element_type=F32)


def tn(a, b):
    return lax.dot_general(a, b, (((0,), (0,)), ((), ())), preferred_element_type=F32)


def normalize(values):
    centred = values - jnp.mean(values, axis=-1, keepdims=True)
    inv_scale = lax.rsqrt(jnp.mean(centred * centred, axis=-1, keepdims=True) + EPSILON)
    return centred * inv_scale, inv_scale


def norm_back(grad_norm, normed_v, inv_scale):
    first = jnp.mean(grad_norm, axis=-1, keepdims=True)
    second = jnp.mean(grad_norm * normed_v, axis=-1, keepdims=True)
    return inv_scale * (grad_norm - first - normed_v * second)


def slot_map(shape, token_dim, live):
    token = lax.broadcasted_iota(jnp.int32, shape, token_dim)
    row = lax.broadcasted_iota(jnp.int32, shape, 1 - token_dim) & (LANES - 1)
    slot = token >> 4
    group = ((token >> 3) & 1) * 2 + ((token >> 1) & 1)
    return jnp.where(slot < live, row - slot * 4 - group, -1)


def select(mapped, shift):
    return jnp.where(mapped == shift, 0.25, 0.0).astype(BF)


def head_rows(block):
    lane = lax.broadcasted_iota(jnp.int32, (1, block.shape[1]), 1)
    parts = []
    for head in range(HEADS):
        mine = (lane >= head * HEAD_DIM) & (lane < (head + 1) * HEAD_DIM)
        parts.append(block * jnp.where(mine, 1.0, 0.0).astype(BF))
    return jnp.concatenate(parts, axis=0)


def heads_to_lanes(rows):
    return jnp.concatenate([rows[h * BLK : (h + 1) * BLK] for h in range(HEADS)], axis=1)


def split(values):
    high = values.astype(BF)
    return high, (values - high.astype(F32)).astype(BF)


def scores_back(att, g_att, keys):
    inner = jnp.sum(g_att * att, axis=keys, keepdims=True)
    return (att * (g_att - inner) * HEAD_DIM ** (-0.5)).astype(BF)


def gain_rows(total):
    row = lax.broadcasted_iota(jnp.int32, (32, LANES), 0)
    last = jnp.concatenate([total[:, 256:], jnp.zeros((1, 96), F32)], axis=1)
    out = jnp.where(row == 0, total[:, :128], 0.0)
    out = jnp.where(row == 1, total[:, 128:256], out)
    return jnp.where(row == 2, last, out).astype(BF)


def main_kernel(
    live_ref, tok_hbm, cot_hbm, w_qkv_hbm, w_out_hbm, w_pool_hbm, gain_one_hbm, gain_two_hbm,
    f_ref, pooled_out, grad_tokens_ref,
    tok_ref, cot_ref, w_qkv_ref, w_out_ref, w_pool_ref, gain_one_ref, gain_two_ref,
    counts_ref, cots_ref, pooled_ref, prev_ref, g_ref, n_one_ref, n_two_ref, gr_ref, qkv_ref, mixed_ref, gqkv_ref, gmix_ref, to_rows, to_tokens, h_rows,
    att_ref, att_t, q_rows, k_rows, normed_t, mixed_t, r_one, s_ref, r_two, t_ref, r_three, u_ref, line_ready,
    in_sems, count_sems, cot_sems, pool_sems, one_send, one_recv, two_send, two_recv, three_send, three_recv,
    five_send, five_recv, six_send, six_recv, line_send,
):
    rows, width = tok_ref.shape
    crows = cots_ref.shape[0] // 2
    out_slots = crows // 4
    factor = HEAD_DIM ** (-0.5)
    blocks = rows // BLK
    me = lax.axis_index("unit")
    z = lax.axis_index("img")
    units = lax.axis_size("unit")
    nz = lax.axis_size("img")
    chips = units // 2
    nx = min(4, chips)
    ny = chips // nx
    core = lax.rem(me, 2)
    chip = me // 2
    chip_x, chip_y = lax.rem(chip, nx), chip // nx
    half = HALF // 2
    piece = half // chips
    tile = piece // 4
    sibling = me + 1 - 2 * core
    plane = [(dx, dy) for dx in AROUND[nx] for dy in AROUND[ny]][:-1]

    swap = core if nx == ny else 0

    def chip_at(dx, dy):
        dx, dy = dx + swap * (dy - dx), dy + swap * (dx - dy)
        return lax.rem(chip_y + dy, ny) * nx + lax.rem(chip_x + dx, nx)

    def fetch(k, source, target):
        copy = pltpu.make_async_copy(source, target, in_sems.at[k])
        copy.start()
        return copy

    def push(source, target, send, recv, **where):
        copy = pltpu.make_async_remote_copy(
            src_ref=source, dst_ref=target, send_sem=send, recv_sem=recv, device_id=where, device_id_type=MESH
        )
        copy.start()
        return copy

    def drain(ref, sem):
        pltpu.make_async_copy(ref, ref, sem).wait()

    barrier = pltpu.get_barrier_semaphore()
    reach = nz // 4
    near = [d for d in range(1, nz) if min(d, nz - d) <= reach]
    for d in near:
        pl.semaphore_signal(barrier, inc=1, device_id={"img": lax.rem(z + d, nz)}, device_id_type=MESH)
    for dx, dy in plane:
        for which in range(2):
            there = chip_at(dx, dy) * 2 + which
            pl.semaphore_signal(barrier, inc=1, device_id={"unit": there}, device_id_type=MESH)
    pl.semaphore_signal(barrier, inc=1, device_id={"unit": sibling}, device_id_type=MESH)

    get_tok = fetch(0, tok_hbm, tok_ref)
    get_gain_one = fetch(1, gain_one_hbm, gain_one_ref)
    get_w_qkv = fetch(2, w_qkv_hbm, w_qkv_ref)
    get_cot = fetch(3, cot_hbm, cot_ref)
    get_w_out = fetch(4, w_out_hbm, w_out_ref)
    get_gain_two = fetch(5, gain_two_hbm, gain_two_ref)
    get_w_pool = fetch(6, w_pool_hbm, w_pool_ref)

    def half_of(part, which):
        return pl.ds(pl.multiple_of(part * HALF + which * half, half), half)

    def pair_send(part):
        count = half - 32 * part
        push(
            g_ref.at[pl.ds(pl.multiple_of(part * HALF + (1 - core) * half, half), count)],
            r_one.at[part, pl.ds(0, count)], one_send.at[part], one_recv.at[part], unit=sibling,
        )

    def pair_send_last():
        start = HALF + (1 - core) * half + half - 32
        push(
            g_ref.at[pl.ds(pl.multiple_of(start, 32), 32)], r_one.at[1, pl.ds(half - 32, 32)],
            one_send.at[2], one_recv.at[2], unit=sibling,
        )

    def pair_add(part):
        drain(r_one.at[part, pl.ds(0, half - 32 * part)], one_recv.at[part])
        if part == 1:
            drain(r_one.at[1, pl.ds(half - 32, 32)], one_recv.at[2])
        own = g_ref[half_of(part, core), :]
        s_ref[part] = (own.astype(F32) + r_one[part].astype(F32)).astype(BF)
        for k, (dx, dy) in enumerate(plane):
            there = chip_at(dx, dy)
            push(
                s_ref.at[part, pl.ds(pl.multiple_of(there * piece, piece), piece)], r_two.at[part, k],
                two_send.at[part], two_recv.at[part], unit=there * 2 + core,
            )

    def plane_add(part):
        drain(r_two.at[part], two_recv.at[part])
        total = s_ref[part, pl.ds(pl.multiple_of(chip * piece, piece), piece), :].astype(F32)
        for k in range(chips - 1):
            total = total + r_two[part, k].astype(F32)
        t_ref[part] = total.astype(BF)
        for d in sorted(range(1, nz), key=lambda d: -min(d, nz - d)):
            there = lax.rem(z + d, nz)
            push(
                t_ref.at[part, pl.ds(pl.multiple_of(lax.rem(there, 4) * tile, tile), tile)], r_three.at[part, z],
                three_send.at[part], three_recv.at[part], img=there,
            )
        r_three[part, z] = t_ref[part, pl.ds(pl.multiple_of(lax.rem(z, 4) * tile, tile), tile), :]

    mine = pl.ds(pl.multiple_of(lax.rem(z, 4) * tile, tile), tile)

    def place(part, which_core, which_chip):
        return pl.ds(pl.multiple_of(part * HALF + which_core * half + which_chip * piece, piece), piece)

    def line_add(part):
        drain(r_three.at[part, pl.ds(0, nz - 1)], three_recv.at[part])
        total = r_three[part, 0].astype(F32)
        for k in range(1, nz):
            total = total + r_three[part, k].astype(F32)
        u_ref[part] = total.astype(BF)
        start = part * HALF + core * half + chip * piece + lax.rem(z, 4) * tile
        here = pl.ds(pl.multiple_of(start, tile), tile)
        if part == 0:
            for d in (2, 1, nz - 1):
                push(
                    u_ref.at[part], f_ref.at[here], line_send, five_recv.at[part, chips - 1],
                    img=lax.rem(z + d, nz),
                )
            f_ref[here, :] = u_ref[part]
            return
        for k, (dx, dy) in enumerate(plane + [(0, 0)]):
            for d in (2, 1, nz - 1, 0):
                if k < chips - 1 or d > 0:
                    push(
                        u_ref.at[part], f_ref.at[here], five_send.at[part], five_recv.at[part, k],
                        img=lax.rem(z + d, nz), unit=chip_at(dx, dy) * 2 + core,
                    )
        f_ref[here, :] = u_ref[part]

    def plane_spread(part):
        drain(f_ref.at[pl.ds(0, 3 * tile)], five_recv.at[part, chips - 1])
        own = f_ref.at[place(part, core, chip)]
        for k, (dx, dy) in enumerate(plane):
            push(own, own, five_send.at[part], five_recv.at[part, k], unit=chip_at(dx, dy) * 2 + core)

    def pair_spread(part):
        for k, (dx, dy) in reversed(list(enumerate(plane + [(0, 0)]))):
            there = place(part, core, chip_at(nx - dx, ny - dy))
            if k < chips - 1:
                drain(f_ref.at[there], five_recv.at[part, k])
            elif part == 1:
                drain(f_ref.at[pl.ds(0, 3 * tile)], five_recv.at[part, k])
            push(f_ref.at[there], f_ref.at[there], six_send.at[part], six_recv.at[part], unit=sibling)

    get_tok.wait()
    get_gain_one.wait()
    n_one, p_one = normalize(tok_ref[...].astype(F32))
    n_one_ref[...] = n_one
    normed = (n_one * gain_one_ref[...]).astype(BF)
    get_w_qkv.wait()
    qkv_ref[...] = nn(normed, w_qkv_ref[...]).astype(BF)

    get_cot.wait()
    cots_ref[:crows, :] = cot_ref[...].reshape(crows, cots_ref.shape[1])
    counts_ref[me] = jnp.full((1, LANES), live_ref[0, 0], jnp.int32)
    pl.semaphore_wait(barrier, len(near) + units - 1)
    for d in (reach, nz - reach):
        pl.semaphore_signal(line_ready, inc=1, device_id={"img": lax.rem(z + d, nz)}, device_id_type=MESH)
    for dx, dy in plane:
        for which in range(2):
            there = chip_at(dx, dy) * 2 + which
            push(counts_ref.at[me], counts_ref.at[me], count_sems.at[0], count_sems.at[1], unit=there)
    push(counts_ref.at[me], counts_ref.at[me], count_sems.at[0], count_sems.at[1], unit=sibling)
    cot_copy = push(
        cots_ref.at[pl.ds(0, crows)], cots_ref.at[pl.ds(crows, crows)], cot_sems.at[0], cot_sems.at[1],
        unit=lax.rem(me + units - 1, units),
    )

    same = (
        lax.broadcasted_iota(jnp.int32, (HEADS * BLK, BLK), 0) & (BLK - 1)
    ) >> 4 == lax.broadcasted_iota(jnp.int32, (HEADS * BLK, BLK), 1) >> 4
    for b in range(blocks):
        span = slice(b * BLK, (b + 1) * BLK)
        q_rows[b] = head_rows(qkv_ref[span, :width])
        k_rows[b] = head_rows(qkv_ref[span, width : 2 * width])
        scores = nt(q_rows[b], qkv_ref[span, width : 2 * width]) * factor
        scores = jnp.where(same, scores, -1e30)
        e = jnp.exp(scores - jnp.max(scores, axis=-1, keepdims=True))
        att = e * (1.0 / jnp.sum(e, axis=-1, keepdims=True))
        att_ref[b] = att
        att_t[b] = att.astype(BF).T
        value = head_rows(qkv_ref[span, 2 * width :])
        mixed_ref[span, :] = nn(heads_to_lanes(att.astype(BF)), value).astype(BF)
    normed_t[...] = normed.T

    get_w_out.wait()
    get_gain_two.wait()
    n_two, p_two = normalize(tok_ref[...].astype(F32) + nn(mixed_ref[...], w_out_ref[...]))
    n_two_ref[...] = n_two
    high, low = split(n_two)
    mixed_t[...] = mixed_ref[...].T
    live = live_ref[0, 0]
    to_rows[...] = slot_map(to_rows.shape, 1, live)
    to_tokens[...] = slot_map(to_tokens.shape, 0, live)
    get_w_pool.wait()
    cot_copy.wait_recv()
    cots = cots_ref[...]
    g_grouped = nt(cots, w_pool_ref[...])
    h_grouped = g_grouped * gain_two_ref[...]
    h_high, h_low = split(h_grouped - jnp.mean(h_grouped, axis=-1, keepdims=True))
    gap = jnp.zeros((LANES - h_high.shape[0], width), BF)
    h_rows[...] = jnp.concatenate([h_high, gap, h_low, gap], axis=0)

    others = counts_ref.at[pl.ds(0, units - 1)]
    drain(others, count_sems.at[1])
    before = jnp.zeros((1, LANES), jnp.int32)
    for k in range(units):
        before = before + jnp.where(k < me, counts_ref[k], 0)
    shift = (before[:, 0:1] - me * out_slots) * 4

    h = nn(select(to_tokens[...], shift), h_rows[...])
    n_two = n_two_ref[...]
    g_resid = p_two * (h - n_two * jnp.mean(h * n_two, axis=-1, keepdims=True))
    gr_ref[...] = g_resid
    resid_b = g_resid.astype(BF)

    gather = select(to_rows[...], shift)
    mean_two = nn(gather, high) + nn(gather, low)
    grouped = (mean_two * gain_two_ref[...]).astype(BF)
    g_ref[2016:2048, :] = gain_rows(jnp.sum(g_grouped * mean_two, axis=0, keepdims=True))
    grad_pool = tn(grouped, cots).astype(BF)
    grad_out = nn(mixed_t[...], resid_b).astype(BF)
    for k in range(4):
        g_ref[width * k : width * (k + 1), :] = grad_pool[:, LANES * k : LANES * (k + 1)]
    g_ref[width * 4 : width * 5, :] = jnp.concatenate(
        [grad_pool[:, 512:576], grad_out[:, 256:288], jnp.zeros((width, 32), BF)], axis=1
    )
    g_ref[width * 5 : width * 6, :] = grad_out[:, :128]
    g_ref[width * 6 : width * 7, :] = grad_out[:, 128:256]
    pair_send(0)

    gmix_ref[...] = nt(resid_b, w_out_ref[...]).astype(BF)

    def scores_of(b):
        span = slice(b * BLK, (b + 1) * BLK)
        rows_b = head_rows(gmix_ref[span, :])
        return rows_b, nt(rows_b, qkv_ref[span, 2 * width :])

    ahead = scores_of(0)
    for b in range(blocks):
        span = slice(b * BLK, (b + 1) * BLK)
        g_mixed, g_att = ahead
        if b + 1 < blocks:
            ahead = scores_of(b + 1)
        g_value = nn(att_t[b], g_mixed).astype(BF)
        g_scores = scores_back(att_ref[b], g_att, -1)
        g_query = nn(heads_to_lanes(g_scores), k_rows[b]).astype(BF)
        g_key = tn(g_scores, q_rows[b]).astype(BF)
        gqkv_ref[span, :] = jnp.concatenate([g_query, g_key, g_value], axis=1)
        if b == 0:
            pair_add(0)

    g_qkv = gqkv_ref[...]
    n_one = n_one_ref[...]
    grad_qkv = nn(normed_t[...], g_qkv).astype(BF)
    for k in range(6):
        g_ref[HALF + width * k : HALF + width * (k + 1), :] = grad_qkv[:, LANES * k : LANES * (k + 1)]
    g_ref[HALF + width * 6 : HALF + width * 7, :] = jnp.concatenate(
        [grad_qkv[:, 768:864], jnp.zeros((width, 32), BF)], axis=1
    )
    pair_send(1)
    g_normed = nt(g_qkv, w_qkv_ref[...])
    g_ref[HALF + 2016 : HALF + 2048, :] = gain_rows(jnp.sum(g_normed * n_one, axis=0, keepdims=True))
    pair_send_last()
    pooled_ref[...] = nn(grouped, w_pool_ref[...]).astype(BF)
    pooled_copy = push(
        pooled_ref.at[pl.ds(crows, crows)], prev_ref, pool_sems.at[0], pool_sems.at[1],
        unit=lax.rem(me + 1, units),
    )
    g_input = norm_back(g_normed * gain_one_ref[...], n_one, p_one)
    grad_tokens_ref[...] = (gr_ref[...] + g_input).astype(BF)

    pair_add(1)
    pl.semaphore_wait(line_ready, 2)
    plane_add(0)
    plane_add(1)
    line_add(0)
    plane_spread(0)
    line_add(1)
    pooled_copy.wait_recv()
    pooled_out[...] = pooled_ref[:crows, :] + prev_ref[...]
    pair_spread(0)
    pair_spread(1)

    for part in range(2):
        drain(g_ref.at[pl.ds(0, half - 32 * part)], one_send.at[part])
        drain(r_two.at[part], two_send.at[part])
        drain(r_three.at[part, pl.ds(0, nz - 1)], three_send.at[part])
        drain(f_ref.at[pl.ds(0, half - (piece, tile)[part])], five_send.at[part])
        drain(f_ref.at[pl.ds(0, half)], six_send.at[part])
        drain(f_ref.at[pl.ds(0, half)], six_recv.at[part])
    drain(g_ref.at[pl.ds(0, 32)], one_send.at[2])
    drain(f_ref.at[pl.ds(0, 3 * tile)], line_send)
    drain(others, count_sems.at[0])
    cot_copy.wait_send()
    pooled_copy.wait_send()


def unpack_kernel(
    scale, f_ref, pooled_ref, tok_ref, out_hbm, grad_tokens_hbm, qkv_hbm, go_hbm, pool_hbm, one_hbm, two_hbm,
    out_ref, qkv_ref, go_ref, pool_ref, one_ref, two_ref, sems,
):
    width = go_ref.shape[0]
    copies = []

    def store(source, target):
        copy = pltpu.make_async_copy(source, target, sems.at[len(copies)])
        copy.start()
        copies.append(copy)

    store(tok_ref, grad_tokens_hbm)
    step = width // 3
    for r in range(0, width, step):
        span = slice(r, r + step)

        def rows(start):
            return f_ref[start + r : start + r + step, :].astype(F32) * scale

        for k in range(6):
            qkv_ref[span, LANES * k : LANES * (k + 1)] = rows(HALF + width * k)
        qkv_ref[span, 768:864] = rows(HALF + width * 6)[:, :96]
        store(qkv_ref.at[pl.ds(r, step)], qkv_hbm.at[pl.ds(r, step)])
        for k in range(4):
            pool_ref[span, LANES * k : LANES * (k + 1)] = rows(width * k)
        both = rows(width * 4)
        pool_ref[span, 512:576] = both[:, :64]
        store(pool_ref.at[pl.ds(r, step)], pool_hbm.at[pl.ds(r, step)])
        go_ref[span, 256:288] = both[:, 64:96]
        for k in range(2):
            go_ref[span, LANES * k : LANES * (k + 1)] = rows(width * (k + 5))
        store(go_ref.at[pl.ds(r, step)], go_hbm.at[pl.ds(r, step)])
    for start, ref, target in ((2016, two_ref, two_hbm), (HALF + 2016, one_ref, one_hbm)):
        last = f_ref[start : start + 32, :].astype(F32) * scale
        ref[...] = jnp.concatenate([last[0:1], last[1:2], last[2:3, :32]], axis=1).reshape(ref.shape)
        store(ref, target)
    out_ref[...] = pooled_ref[...].reshape(out_ref.shape)
    store(out_ref, out_hbm)
    for copy in copies:
        copy.wait()


def whole(count, space=pltpu.VMEM):
    return [pl.BlockSpec(memory_space=space)] * count


def local(tokens, live, cotangent, w_qkv, w_out, w_pool, gain_one, gain_two):
    img_dev, slots, token_count, width = tokens.shape
    out_slots, out_width = cotangent.shape[1], cotangent.shape[3]
    units, nz = lax.axis_size("unit"), lax.axis_size("img")
    chips = units // 2
    rows = slots * token_count
    crows = out_slots * 4
    piece = HALF // 2 // chips
    dma, vmem = pltpu.SemaphoreType.DMA, pltpu.VMEM

    def sd(shape, dtype):
        return jax.ShapeDtypeStruct(shape, dtype)

    f, pooled, grad_tok = pl.pallas_call(
        main_kernel,
        out_shape=(vmem((2 * HALF, LANES), BF), vmem((crows, out_width), BF), vmem((rows, width), BF)),
        in_specs=[pl.BlockSpec(memory_space=pltpu.SMEM)] + whole(7, pltpu.HBM),
        out_specs=whole(3),
        scratch_shapes=[
            vmem((rows, width), BF),
            vmem((out_slots, 4, out_width), BF),
            vmem(w_qkv.shape, BF),
            vmem(w_out.shape, BF),
            vmem(w_pool.shape, BF),
            vmem(gain_one.shape, F32),
            vmem(gain_two.shape, F32),
            vmem((units, 1, LANES), jnp.int32),
            vmem((2 * crows, out_width), BF),
            vmem((2 * crows, out_width), BF),
            vmem((crows, out_width), BF),
            vmem((2 * HALF, LANES), BF),
            vmem((rows, width), F32),
            vmem((rows, width), F32),
            vmem((rows, width), F32),
            vmem((rows, 3 * width), BF),
            vmem((rows, width), BF),
            vmem((rows, 3 * width), BF),
            vmem((rows, width), BF),
            vmem((2 * crows, rows), jnp.int32),
            vmem((rows, 2 * LANES), jnp.int32),
            vmem((2 * LANES, width), BF),
            vmem((rows // BLK, HEADS * BLK, BLK), F32),
            vmem((rows // BLK, BLK, HEADS * BLK), BF),
            vmem((rows // BLK, HEADS * BLK, width), BF),
            vmem((rows // BLK, HEADS * BLK, width), BF),
            vmem((width, rows), BF),
            vmem((width, rows), BF),
            vmem((2, HALF // 2, LANES), BF),
            vmem((2, HALF // 2, LANES), BF),
            vmem((2, chips - 1, piece, LANES), BF),
            vmem((2, piece, LANES), BF),
            vmem((2, nz, piece // 4, LANES), BF),
            vmem((2, piece // 4, LANES), BF),
            pltpu.SemaphoreType.REGULAR,
            dma((7,)), dma((2,)), dma((2,)), dma((2,)), dma((3,)), dma((3,)), dma((2,)), dma((2,)), dma((2,)),
            dma((2,)), dma((2,)), dma((2, chips)), dma((2,)), dma((2,)), dma,
        ],
        compiler_params=pltpu.CompilerParams(collective_id=0, has_side_effects=True, vmem_limit_bytes=VMEM_LIMIT),
        name="main",
    )(
        live, tokens.reshape(rows, width), cotangent.reshape(out_slots, 4, out_width), w_qkv, w_out, w_pool,
        gain_one, gain_two,
    )

    scale = 1.0 / math.sqrt(img_dev * nz * out_slots * units)
    out, grad_tokens, grad_qkv, grad_out, grad_pool, one, two = pl.pallas_call(
        functools.partial(unpack_kernel, scale),
        out_shape=(
            sd((out_slots, 4, out_width), BF), sd((rows, width), BF), sd((width, 3 * width), F32),
            sd((width, width), F32), sd((width, out_width), F32), sd((width,), F32), sd((width,), F32),
        ),
        in_specs=whole(3),
        out_specs=whole(7, pl.ANY),
        scratch_shapes=[
            vmem((out_slots, 4, out_width), BF), vmem((width, 3 * width), F32), vmem((width, width), F32),
            vmem((width, out_width), F32), vmem((width,), F32), vmem((width,), F32), dma((13,)),
        ],
        compiler_params=pltpu.CompilerParams(vmem_limit_bytes=UNPACK_LIMIT),
        name="unpack",
    )(f, pooled, grad_tok)
    return (
        out.reshape(cotangent.shape), grad_tokens.reshape(tokens.shape), grad_qkv, grad_out, grad_pool, one, two,
    )


def solution(mesh):
    return jax.shard_map(
        local,
        mesh=mesh,
        in_specs=(
            P("img", "unit", None, None), P("img", "unit"), P("img", "unit", None, None),
            P(), P(), P(), P(), P(),
        ),
        out_specs=(P("img", "unit", None, None), P("img", "unit", None, None), P(), P(), P(), P(), P()),
        check_vma=False,
    )
```

```python
import functools
import math

import jax
import jax.numpy as jnp
from jax import lax
from jax.experimental import pallas as pl
from jax.experimental.pallas import tpu as pltpu
from jax.sharding import PartitionSpec as P

HEADS = 4
HEAD_DIM = 72
EPSILON = 1e-06
BF = jnp.bfloat16
F32 = jnp.float32
MESH = pl.DeviceIdType.MESH
TOK = 16
BLK = 128
LANES = 128
HALF = 2048
AROUND = {1: (0,), 2: (1, 0), 4: (2, 1, 3, 0)}
VMEM_LIMIT = 62 * 1024 * 1024
UNPACK_LIMIT = 24 * 1024 * 1024


def nn(a, b):
    return lax.dot_general(a, b, (((1,), (0,)), ((), ())), preferred_element_type=F32)


def nt(a, b):
    return lax.dot_general(a, b, (((1,), (1,)), ((), ())), preferred_element_type=F32)


def tn(a, b):
    return lax.dot_general(a, b, (((0,), (0,)), ((), ())), preferred_element_type=F32)


def normalize(values):
    centred = values - jnp.mean(values, axis=-1, keepdims=True)
    inv_scale = lax.rsqrt(jnp.mean(centred * centred, axis=-1, keepdims=True) + EPSILON)
    return centred * inv_scale, inv_scale


def norm_back(grad_norm, normed_v, inv_scale):
    first = jnp.mean(grad_norm, axis=-1, keepdims=True)
    second = jnp.mean(grad_norm * normed_v, axis=-1, keepdims=True)
    return inv_scale * (grad_norm - first - normed_v * second)


def slot_map(shape, token_dim, live):
    token = lax.broadcasted_iota(jnp.int32, shape, token_dim)
    row = lax.broadcasted_iota(jnp.int32, shape, 1 - token_dim) & (LANES - 1)
    slot = token >> 4
    group = ((token >> 3) & 1) * 2 + ((token >> 1) & 1)
    return jnp.where(slot < live, row - slot * 4 - group, -1)


def select(mapped, shift):
    return jnp.where(mapped == shift, 0.25, 0.0).astype(BF)


def head_rows(block):
    lane = lax.broadcasted_iota(jnp.int32, (1, block.shape[1]), 1)
    parts = []
    for head in range(HEADS):
        mine = (lane >= head * HEAD_DIM) & (lane < (head + 1) * HEAD_DIM)
        parts.append(block * jnp.where(mine, 1.0, 0.0).astype(BF))
    return jnp.concatenate(parts, axis=0)


def heads_to_lanes(rows):
    return jnp.concatenate([rows[h * BLK : (h + 1) * BLK] for h in range(HEADS)], axis=1)


def split(values):
    high = values.astype(BF)
    return high, (values - high.astype(F32)).astype(BF)


def scores_back(att, g_att, keys):
    inner = jnp.sum(g_att * att, axis=keys, keepdims=True)
    return (att * (g_att - inner) * HEAD_DIM ** (-0.5)).astype(BF)


def gain_rows(total):
    row = lax.broadcasted_iota(jnp.int32, (32, LANES), 0)
    last = jnp.concatenate([total[:, 256:], jnp.zeros((1, 96), F32)], axis=1)
    out = jnp.where(row == 0, total[:, :128], 0.0)
    out = jnp.where(row == 1, total[:, 128:256], out)
    return jnp.where(row == 2, last, out).astype(BF)


def main_kernel(
    live_ref, tok_hbm, cot_hbm, w_qkv_hbm, w_out_hbm, w_pool_hbm, gain_one_hbm, gain_two_hbm,
    f_ref, pooled_out, grad_tokens_ref,
    tok_ref, cot_ref, w_qkv_ref, w_out_ref, w_pool_ref, gain_one_ref, gain_two_ref,
    counts_ref, cots_ref, pooled_ref, prev_ref, g_ref, n_one_ref, n_two_ref, gr_ref, qkv_ref, mixed_ref, gqkv_ref, gmix_ref, to_rows, to_tokens, h_rows,
    att_ref, att_t, q_rows, k_rows, normed_t, mixed_t, r_one, s_ref, r_two, t_ref, r_three, u_ref, line_ready,
    in_sems, count_sems, cot_sems, pool_sems, one_send, one_recv, two_send, two_recv, three_send, three_recv,
    five_send, five_recv, six_send, six_recv, line_send,
):
    rows, width = tok_ref.shape
    crows = cots_ref.shape[0] // 2
    out_slots = crows // 4
    factor = HEAD_DIM ** (-0.5)
    blocks = rows // BLK
    me = lax.axis_index("unit")
    z = lax.axis_index("img")
    units = lax.axis_size("unit")
    nz = lax.axis_size("img")
    chips = units // 2
    nx = min(4, chips)
    ny = chips // nx
    core = lax.rem(me, 2)
    chip = me // 2
    chip_x, chip_y = lax.rem(chip, nx), chip // nx
    half = HALF // 2
    piece = half // chips
    tile = piece // 4
    sibling = me + 1 - 2 * core
    plane = [(dx, dy) for dx in AROUND[nx] for dy in AROUND[ny]][:-1]

    swap = core if nx == ny else 0

    def chip_at(dx, dy):
        dx, dy = dx + swap * (dy - dx), dy + swap * (dx - dy)
        return lax.rem(chip_y + dy, ny) * nx + lax.rem(chip_x + dx, nx)

    def fetch(k, source, target):
        copy = pltpu.make_async_copy(source, target, in_sems.at[k])
        copy.start()
        return copy

    def push(source, target, send, recv, **where):
        copy = pltpu.make_async_remote_copy(
            src_ref=source, dst_ref=target, send_sem=send, recv_sem=recv, device_id=where, device_id_type=MESH
        )
        copy.start()
        return copy

    def drain(ref, sem):
        pltpu.make_async_copy(ref, ref, sem).wait()

    barrier = pltpu.get_barrier_semaphore()
    reach = nz // 4
    near = [d for d in range(1, nz) if min(d, nz - d) <= reach]
    for d in near:
        pl.semaphore_signal(barrier, inc=1, device_id={"img": lax.rem(z + d, nz)}, device_id_type=MESH)
    for dx, dy in plane:
        for which in range(2):
            there = chip_at(dx, dy) * 2 + which
            pl.semaphore_signal(barrier, inc=1, device_id={"unit": there}, device_id_type=MESH)
    pl.semaphore_signal(barrier, inc=1, device_id={"unit": sibling}, device_id_type=MESH)

    get_tok = fetch(0, tok_hbm, tok_ref)
    get_gain_one = fetch(1, gain_one_hbm, gain_one_ref)
    get_w_qkv = fetch(2, w_qkv_hbm, w_qkv_ref)
    get_cot = fetch(3, cot_hbm, cot_ref)
    get_w_out = fetch(4, w_out_hbm, w_out_ref)
    get_gain_two = fetch(5, gain_two_hbm, gain_two_ref)
    get_w_pool = fetch(6, w_pool_hbm, w_pool_ref)

    def half_of(part, which):
        return pl.ds(pl.multiple_of(part * HALF + which * half, half), half)

    def pair_send(part):
        count = half - 32 * part
        push(
            g_ref.at[pl.ds(pl.multiple_of(part * HALF + (1 - core) * half, half), count)],
            r_one.at[part, pl.ds(0, count)], one_send.at[part], one_recv.at[part], unit=sibling,
        )

    def pair_send_last():
        start = HALF + (1 - core) * half + half - 32
        push(
            g_ref.at[pl.ds(pl.multiple_of(start, 32), 32)], r_one.at[1, pl.ds(half - 32, 32)],
            one_send.at[2], one_recv.at[2], unit=sibling,
        )

    def pair_add(part):
        drain(r_one.at[part, pl.ds(0, half - 32 * part)], one_recv.at[part])
        if part == 1:
            drain(r_one.at[1, pl.ds(half - 32, 32)], one_recv.at[2])
        own = g_ref[half_of(part, core), :]
        s_ref[part] = (own.astype(F32) + r_one[part].astype(F32)).astype(BF)
        for k, (dx, dy) in enumerate(plane):
            there = chip_at(dx, dy)
            push(
                s_ref.at[part, pl.ds(pl.multiple_of(there * piece, piece), piece)], r_two.at[part, k],
                two_send.at[part], two_recv.at[part], unit=there * 2 + core,
            )

    def plane_add(part):
        drain(r_two.at[part], two_recv.at[part])
        total = s_ref[part, pl.ds(pl.multiple_of(chip * piece, piece), piece), :].astype(F32)
        for k in range(chips - 1):
            total = total + r_two[part, k].astype(F32)
        t_ref[part] = total.astype(BF)
        for d in sorted(range(1, nz), key=lambda d: -min(d, nz - d)):
            there = lax.rem(z + d, nz)
            push(
                t_ref.at[part, pl.ds(pl.multiple_of(lax.rem(there, 4) * tile, tile), tile)], r_three.at[part, z],
                three_send.at[part], three_recv.at[part], img=there,
            )
        r_three[part, z] = t_ref[part, pl.ds(pl.multiple_of(lax.rem(z, 4) * tile, tile), tile), :]

    mine = pl.ds(pl.multiple_of(lax.rem(z, 4) * tile, tile), tile)

    def place(part, which_core, which_chip):
        return pl.ds(pl.multiple_of(part * HALF + which_core * half + which_chip * piece, piece), piece)

    def line_add(part):
        drain(r_three.at[part, pl.ds(0, nz - 1)], three_recv.at[part])
        total = r_three[part, 0].astype(F32)
        for k in range(1, nz):
            total = total + r_three[part, k].astype(F32)
        u_ref[part] = total.astype(BF)
        start = part * HALF + core * half + chip * piece + lax.rem(z, 4) * tile
        here = pl.ds(pl.multiple_of(start, tile), tile)
        if part == 0:
            for d in (2, 1, nz - 1):
                push(
                    u_ref.at[part], f_ref.at[here], line_send, five_recv.at[part, chips - 1],
                    img=lax.rem(z + d, nz),
                )
            f_ref[here, :] = u_ref[part]
            return
        for k, (dx, dy) in enumerate(plane + [(0, 0)]):
            for d in (2, 1, nz - 1, 0):
                if k < chips - 1 or d > 0:
                    push(
                        u_ref.at[part], f_ref.at[here], five_send.at[part], five_recv.at[part, k],
                        img=lax.rem(z + d, nz), unit=chip_at(dx, dy) * 2 + core,
                    )
        f_ref[here, :] = u_ref[part]

    def plane_spread(part):
        drain(f_ref.at[pl.ds(0, 3 * tile)], five_recv.at[part, chips - 1])
        own = f_ref.at[place(part, core, chip)]
        for k, (dx, dy) in enumerate(plane):
            push(own, own, five_send.at[part], five_recv.at[part, k], unit=chip_at(dx, dy) * 2 + core)

    def pair_spread(part):
        for k, (dx, dy) in reversed(list(enumerate(plane + [(0, 0)]))):
            there = place(part, core, chip_at(nx - dx, ny - dy))
            if k < chips - 1:
                drain(f_ref.at[there], five_recv.at[part, k])
            elif part == 1:
                drain(f_ref.at[pl.ds(0, 3 * tile)], five_recv.at[part, k])
            push(f_ref.at[there], f_ref.at[there], six_send.at[part], six_recv.at[part], unit=sibling)

    get_tok.wait()
    get_gain_one.wait()
    n_one, p_one = normalize(tok_ref[...].astype(F32))
    n_one_ref[...] = n_one
    normed = (n_one * gain_one_ref[...]).astype(BF)
    get_w_qkv.wait()
    qkv_ref[...] = nn(normed, w_qkv_ref[...]).astype(BF)

    same = (
        lax.broadcasted_iota(jnp.int32, (HEADS * BLK, BLK), 0) & (BLK - 1)
    ) >> 4 == lax.broadcasted_iota(jnp.int32, (HEADS * BLK, BLK), 1) >> 4
    for b in range(blocks):
        span = slice(b * BLK, (b + 1) * BLK)
        q_rows[b] = head_rows(qkv_ref[span, :width])
        k_rows[b] = head_rows(qkv_ref[span, width : 2 * width])
        scores = nt(q_rows[b], qkv_ref[span, width : 2 * width]) * factor
        scores = jnp.where(same, scores, -1e30)
        e = jnp.exp(scores - jnp.max(scores, axis=-1, keepdims=True))
        att = e * (1.0 / jnp.sum(e, axis=-1, keepdims=True))
        att_ref[b] = att
        att_t[b] = att.astype(BF).T
        value = head_rows(qkv_ref[span, 2 * width :])
        mixed_ref[span, :] = nn(heads_to_lanes(att.astype(BF)), value).astype(BF)
        if b == 1:
            get_cot.wait()
            cots_ref[:crows, :] = cot_ref[...].reshape(crows, cots_ref.shape[1])
            counts_ref[me] = jnp.full((1, LANES), live_ref[0, 0], jnp.int32)
            pl.semaphore_wait(barrier, len(near) + units - 1)
            for d in (reach, nz - reach):
                pl.semaphore_signal(line_ready, inc=1, device_id={"img": lax.rem(z + d, nz)}, device_id_type=MESH)
            cot_copy = push(
                cots_ref.at[pl.ds(0, crows)], cots_ref.at[pl.ds(crows, crows)], cot_sems.at[0], cot_sems.at[1],
                unit=lax.rem(me + units - 1, units),
            )
            for dx, dy in plane:
                for which in range(2):
                    there = chip_at(dx, dy) * 2 + which
                    push(counts_ref.at[me], counts_ref.at[me], count_sems.at[0], count_sems.at[1], unit=there)
            push(counts_ref.at[me], counts_ref.at[me], count_sems.at[0], count_sems.at[1], unit=sibling)
    normed_t[...] = normed.T

    get_w_out.wait()
    get_gain_two.wait()
    n_two, p_two = normalize(tok_ref[...].astype(F32) + nn(mixed_ref[...], w_out_ref[...]))
    n_two_ref[...] = n_two
    high, low = split(n_two)
    mixed_t[...] = mixed_ref[...].T
    live = live_ref[0, 0]
    to_rows[...] = slot_map(to_rows.shape, 1, live)
    to_tokens[...] = slot_map(to_tokens.shape, 0, live)
    get_w_pool.wait()
    cot_copy.wait_recv()
    cots = cots_ref[...]
    g_grouped = nt(cots, w_pool_ref[...])
    h_grouped = g_grouped * gain_two_ref[...]
    h_high, h_low = split(h_grouped - jnp.mean(h_grouped, axis=-1, keepdims=True))
    gap = jnp.zeros((LANES - h_high.shape[0], width), BF)
    h_rows[...] = jnp.concatenate([h_high, gap, h_low, gap], axis=0)

    others = counts_ref.at[pl.ds(0, units - 1)]
    drain(others, count_sems.at[1])
    before = jnp.zeros((1, LANES), jnp.int32)
    for k in range(units):
        before = before + jnp.where(k < me, counts_ref[k], 0)
    shift = (before[:, 0:1] - me * out_slots) * 4

    h = nn(select(to_tokens[...], shift), h_rows[...])
    n_two = n_two_ref[...]
    g_resid = p_two * (h - n_two * jnp.mean(h * n_two, axis=-1, keepdims=True))
    gr_ref[...] = g_resid
    resid_b = g_resid.astype(BF)

    gather = select(to_rows[...], shift)
    mean_two = nn(gather, high) + nn(gather, low)
    grouped = (mean_two * gain_two_ref[...]).astype(BF)
    g_ref[2016:2048, :] = gain_rows(jnp.sum(g_grouped * mean_two, axis=0, keepdims=True))
    grad_pool = tn(grouped, cots).astype(BF)
    grad_out = nn(mixed_t[...], resid_b).astype(BF)
    for k in range(4):
        g_ref[width * k : width * (k + 1), :] = grad_pool[:, LANES * k : LANES * (k + 1)]
    g_ref[width * 4 : width * 5, :] = jnp.concatenate(
        [grad_pool[:, 512:576], grad_out[:, 256:288], jnp.zeros((width, 32), BF)], axis=1
    )
    g_ref[width * 5 : width * 6, :] = grad_out[:, :128]
    g_ref[width * 6 : width * 7, :] = grad_out[:, 128:256]
    pair_send(0)

    gmix_ref[...] = nt(resid_b, w_out_ref[...]).astype(BF)

    def scores_of(b):
        span = slice(b * BLK, (b + 1) * BLK)
        rows_b = head_rows(gmix_ref[span, :])
        return rows_b, nt(rows_b, qkv_ref[span, 2 * width :])

    ahead = scores_of(0)
    for b in range(blocks):
        span = slice(b * BLK, (b + 1) * BLK)
        g_mixed, g_att = ahead
        if b + 1 < blocks:
            ahead = scores_of(b + 1)
        g_value = nn(att_t[b], g_mixed).astype(BF)
        g_scores = scores_back(att_ref[b], g_att, -1)
        g_query = nn(heads_to_lanes(g_scores), k_rows[b]).astype(BF)
        g_key = tn(g_scores, q_rows[b]).astype(BF)
        gqkv_ref[span, :] = jnp.concatenate([g_query, g_key, g_value], axis=1)
        if b == 0:
            pair_add(0)

    g_qkv = gqkv_ref[...]
    n_one = n_one_ref[...]
    grad_qkv = nn(normed_t[...], g_qkv).astype(BF)
    for k in range(6):
        g_ref[HALF + width * k : HALF + width * (k + 1), :] = grad_qkv[:, LANES * k : LANES * (k + 1)]
    g_ref[HALF + width * 6 : HALF + width * 7, :] = jnp.concatenate(
        [grad_qkv[:, 768:864], jnp.zeros((width, 32), BF)], axis=1
    )
    pair_send(1)
    g_normed = nt(g_qkv, w_qkv_ref[...])
    g_ref[HALF + 2016 : HALF + 2048, :] = gain_rows(jnp.sum(g_normed * n_one, axis=0, keepdims=True))
    pair_send_last()
    pair_add(1)
    pooled_ref[...] = nn(grouped, w_pool_ref[...]).astype(BF)
    pooled_copy = push(
        pooled_ref.at[pl.ds(crows, crows)], prev_ref, pool_sems.at[0], pool_sems.at[1],
        unit=lax.rem(me + 1, units),
    )
    g_input = norm_back(g_normed * gain_one_ref[...], n_one, p_one)
    grad_tokens_ref[...] = (gr_ref[...] + g_input).astype(BF)

    pl.semaphore_wait(line_ready, 2)
    plane_add(0)
    plane_add(1)
    line_add(0)
    plane_spread(0)
    line_add(1)
    pooled_copy.wait_recv()
    pooled_out[...] = pooled_ref[:crows, :] + prev_ref[...]
    pair_spread(0)
    pair_spread(1)

    for part in range(2):
        drain(g_ref.at[pl.ds(0, half - 32 * part)], one_send.at[part])
        drain(r_two.at[part], two_send.at[part])
        drain(r_three.at[part, pl.ds(0, nz - 1)], three_send.at[part])
        drain(f_ref.at[pl.ds(0, half - (piece, tile)[part])], five_send.at[part])
        drain(f_ref.at[pl.ds(0, half)], six_send.at[part])
        drain(f_ref.at[pl.ds(0, half)], six_recv.at[part])
    drain(g_ref.at[pl.ds(0, 32)], one_send.at[2])
    drain(f_ref.at[pl.ds(0, 3 * tile)], line_send)
    drain(others, count_sems.at[0])
    cot_copy.wait_send()
    pooled_copy.wait_send()


def unpack_kernel(
    scale, f_ref, pooled_ref, tok_ref, out_hbm, grad_tokens_hbm, qkv_hbm, go_hbm, pool_hbm, one_hbm, two_hbm,
    out_ref, qkv_ref, go_ref, pool_ref, one_ref, two_ref, sems,
):
    width = go_ref.shape[0]
    copies = []

    def store(source, target):
        copy = pltpu.make_async_copy(source, target, sems.at[len(copies)])
        copy.start()
        copies.append(copy)

    store(tok_ref, grad_tokens_hbm)
    step = width // 3
    for r in range(0, width, step):
        span = slice(r, r + step)

        def rows(start):
            return f_ref[start + r : start + r + step, :].astype(F32) * scale

        for k in range(6):
            qkv_ref[span, LANES * k : LANES * (k + 1)] = rows(HALF + width * k)
        qkv_ref[span, 768:864] = rows(HALF + width * 6)[:, :96]
        store(qkv_ref.at[pl.ds(r, step)], qkv_hbm.at[pl.ds(r, step)])
        for k in range(4):
            pool_ref[span, LANES * k : LANES * (k + 1)] = rows(width * k)
        both = rows(width * 4)
        pool_ref[span, 512:576] = both[:, :64]
        store(pool_ref.at[pl.ds(r, step)], pool_hbm.at[pl.ds(r, step)])
        go_ref[span, 256:288] = both[:, 64:96]
        for k in range(2):
            go_ref[span, LANES * k : LANES * (k + 1)] = rows(width * (k + 5))
        store(go_ref.at[pl.ds(r, step)], go_hbm.at[pl.ds(r, step)])
    for start, ref, target in ((2016, two_ref, two_hbm), (HALF + 2016, one_ref, one_hbm)):
        last = f_ref[start : start + 32, :].astype(F32) * scale
        ref[...] = jnp.concatenate([last[0:1], last[1:2], last[2:3, :32]], axis=1).reshape(ref.shape)
        store(ref, target)
    out_ref[...] = pooled_ref[...].reshape(out_ref.shape)
    store(out_ref, out_hbm)
    for copy in copies:
        copy.wait()


def whole(count, space=pltpu.VMEM):
    return [pl.BlockSpec(memory_space=space)] * count


def local(tokens, live, cotangent, w_qkv, w_out, w_pool, gain_one, gain_two):
    img_dev, slots, token_count, width = tokens.shape
    out_slots, out_width = cotangent.shape[1], cotangent.shape[3]
    units, nz = lax.axis_size("unit"), lax.axis_size("img")
    chips = units // 2
    rows = slots * token_count
    crows = out_slots * 4
    piece = HALF // 2 // chips
    dma, vmem = pltpu.SemaphoreType.DMA, pltpu.VMEM

    def sd(shape, dtype):
        return jax.ShapeDtypeStruct(shape, dtype)

    f, pooled, grad_tok = pl.pallas_call(
        main_kernel,
        out_shape=(vmem((2 * HALF, LANES), BF), vmem((crows, out_width), BF), vmem((rows, width), BF)),
        in_specs=[pl.BlockSpec(memory_space=pltpu.SMEM)] + whole(7, pltpu.HBM),
        out_specs=whole(3),
        scratch_shapes=[
            vmem((rows, width), BF),
            vmem((out_slots, 4, out_width), BF),
            vmem(w_qkv.shape, BF),
            vmem(w_out.shape, BF),
            vmem(w_pool.shape, BF),
            vmem(gain_one.shape, F32),
            vmem(gain_two.shape, F32),
            vmem((units, 1, LANES), jnp.int32),
            vmem((2 * crows, out_width), BF),
            vmem((2 * crows, out_width), BF),
            vmem((crows, out_width), BF),
            vmem((2 * HALF, LANES), BF),
            vmem((rows, width), F32),
            vmem((rows, width), F32),
            vmem((rows, width), F32),
            vmem((rows, 3 * width), BF),
            vmem((rows, width), BF),
            vmem((rows, 3 * width), BF),
            vmem((rows, width), BF),
            vmem((2 * crows, rows), jnp.int32),
            vmem((rows, 2 * LANES), jnp.int32),
            vmem((2 * LANES, width), BF),
            vmem((rows // BLK, HEADS * BLK, BLK), F32),
            vmem((rows // BLK, BLK, HEADS * BLK), BF),
            vmem((rows // BLK, HEADS * BLK, width), BF),
            vmem((rows // BLK, HEADS * BLK, width), BF),
            vmem((width, rows), BF),
            vmem((width, rows), BF),
            vmem((2, HALF // 2, LANES), BF),
            vmem((2, HALF // 2, LANES), BF),
            vmem((2, chips - 1, piece, LANES), BF),
            vmem((2, piece, LANES), BF),
            vmem((2, nz, piece // 4, LANES), BF),
            vmem((2, piece // 4, LANES), BF),
            pltpu.SemaphoreType.REGULAR,
            dma((7,)), dma((2,)), dma((2,)), dma((2,)), dma((3,)), dma((3,)), dma((2,)), dma((2,)), dma((2,)),
            dma((2,)), dma((2,)), dma((2, chips)), dma((2,)), dma((2,)), dma,
        ],
        compiler_params=pltpu.CompilerParams(collective_id=0, has_side_effects=True, vmem_limit_bytes=VMEM_LIMIT),
        name="main",
    )(
        live, tokens.reshape(rows, width), cotangent.reshape(out_slots, 4, out_width), w_qkv, w_out, w_pool,
        gain_one, gain_two,
    )

    scale = 1.0 / math.sqrt(img_dev * nz * out_slots * units)
    out, grad_tokens, grad_qkv, grad_out, grad_pool, one, two = pl.pallas_call(
        functools.partial(unpack_kernel, scale),
        out_shape=(
            sd((out_slots, 4, out_width), BF), sd((rows, width), BF), sd((width, 3 * width), F32),
            sd((width, width), F32), sd((width, out_width), F32), sd((width,), F32), sd((width,), F32),
        ),
        in_specs=whole(3),
        out_specs=whole(7, pl.ANY),
        scratch_shapes=[
            vmem((out_slots, 4, out_width), BF), vmem((width, 3 * width), F32), vmem((width, width), F32),
            vmem((width, out_width), F32), vmem((width,), F32), vmem((width,), F32), dma((13,)),
        ],
        compiler_params=pltpu.CompilerParams(vmem_limit_bytes=UNPACK_LIMIT),
        name="unpack",
    )(f, pooled, grad_tok)
    return (
        out.reshape(cotangent.shape), grad_tokens.reshape(tokens.shape), grad_qkv, grad_out, grad_pool, one, two,
    )


def solution(mesh):
    return jax.shard_map(
        local,
        mesh=mesh,
        in_specs=(
            P("img", "unit", None, None), P("img", "unit"), P("img", "unit", None, None),
            P(), P(), P(), P(), P(),
        ),
        out_specs=(P("img", "unit", None, None), P("img", "unit", None, None), P(), P(), P(), P(), P()),
        check_vma=False,
    )
```
